32 devices in a mesh: groups: 2 (over y), dp: 2 (over core), space: 8 (over z, x).
Axes of the slice: x: 2, y: 2, z: 4, core: 2. Of those that a mesh axis runs over, the one named last changes fastest.
Arguments:
- samples: bfloat16 [4, 16, 32, 512], P(('groups', 'dp'), 'space'), parts along dimension 0, may hold values from -6 to 6
- cotangent: bfloat16 [4, 16, 32, 512], P(('groups', 'dp'), 'space'), parts along dimension 0, may hold values from -6 to 6
- wave_owner: int32 [16], replicated, may hold values from 0 to 7, as said below
- filter_weight: bfloat16 [2, 16, 512], replicated, may hold values from -4 to 4
- zonal_gain: bfloat16 [2, 16, 512], P(None, 'space'), may hold values from -4 to 4
Outputs:
- sample_grad: bfloat16 [4, 16, 32, 512], P(('groups', 'dp'), 'space'), parts along dimension 0
- weight_grad: bfloat16 [4, 16, 512], P('groups'), parts along dimension 0
- gain_grad: float32 [4, 16, 512], P('groups', 'space'), parts along dimension 0
The draws below stay inside these ranges and needn't reach their ends.
There are 2 independent parts, one for each index of `groups`. The reference program is written for one: setup_inputs(seed, part) draws one part's arguments, and reference() takes and returns one part's arrays. A program takes and returns all parts, laid end to end along the dimension named above; an argument that names none is the same for every part. Nothing has to cross between parts.
Inputs may be any that keep to these rules, and one draw needn't show every extreme that they name: wave_owner[m] equals wave_owner[15 - m], and each index along space owns exactly 2 wavenumbers.
All inputs are finite; a program needn't handle non-finite values.
Results may differ from the reference program's by a relative error of at most 0.011.
Values may be sent and summed in bfloat16 or wider, within the bound.
A program may use at most 64 MiB of HBM per device.

```python
import math
import jax
import jax.numpy as jnp
from jax import lax

C = 512
LAT_DEV = 2
NLAT = 16
NLON = 32
MODES = 16
N_DP = 2
N_SPACE = 8


def draw_wave_owner(key, part):
    key = jax.random.fold_in(key, 11)
    shuffled = jax.random.permutation(key, MODES // 2)
    pair_owner = (shuffled // (LAT_DEV // 2)).astype(jnp.int32)
    wavenum = jnp.arange(MODES, dtype=jnp.int32)
    paired = jnp.minimum(wavenum, MODES - 1 - wavenum)
    return jnp.take(pair_owner, paired).astype(jnp.int32)


def block_levels(key, shape, split, low, largest):
    def one(position, blocks):
        draws = jax.random.uniform(jax.random.fold_in(jax.random.fold_in(key, 6), position), (blocks,), jnp.float32, low / len(split), largest / len(split))
        return jnp.repeat(jnp.exp(draws), shape[position] // blocks).reshape((-1,) + (1,) * (len(shape) - position - 1))

    gain = one(*split[0])
    for cut in split[1:]:
        gain = gain * one(*cut)
    return gain


def gaussian(stream_key, extent, spread, most, split=(), kind=jnp.bfloat16):
    level = block_levels(stream_key, extent, split, -0.22, 0.18) if split else 1.0
    array = jax.random.normal(stream_key, extent, jnp.float32) * spread * level
    return jnp.minimum(jnp.maximum(array, -most), most).astype(kind)


def setup_inputs(seed: int = 0, part: int = 0) -> dict:
    key_of = jax.random.split(jax.random.key(seed), 6)
    part_splits = jax.random.split(jax.random.fold_in(key_of[5], part), 6)
    samples = gaussian(part_splits[0], (N_DP, NLAT, NLON, C), 1.0, 6.0, ((0, 2), (1, 8)))
    cotangent = gaussian(part_splits[1], (N_DP, NLAT, NLON, C), 1.0, 6.0, ((0, 2), (1, 8)))
    wave_owner = draw_wave_owner(jax.random.fold_in(key_of[5], 71), part)
    filter_weight = gaussian(key_of[3], (2, MODES, C), 0.7, 4.0)
    zonal_gain = gaussian(key_of[4], (2, MODES, C), 0.7, 4.0, ((1, 8),))
    return {"samples": samples, "cotangent": cotangent, "wave_owner": wave_owner, "filter_weight": filter_weight, "zonal_gain": zonal_gain}


def slot_tables(wave_owner, per_device, devices):
    is_owner = (wave_owner[:, None] == jnp.arange(devices, dtype=jnp.int32)[None, :]).astype(jnp.int32)
    owner_rank = lax.optimization_barrier(jnp.sum((jnp.cumsum(is_owner, axis=0) - 1) * is_owner, axis=1))
    slot_of = (wave_owner * per_device + owner_rank).astype(jnp.int32)
    total_modes = wave_owner.shape[0]
    positions = jnp.arange(total_modes, dtype=jnp.int32)
    matches = (slot_of[None, :] == positions[:, None]).astype(jnp.int32)
    order_of = lax.optimization_barrier(jnp.sum(matches * positions[None, :], axis=1)).astype(jnp.int32)
    return (slot_of, order_of)

def fourier_table(wavenums, points):
    longitude = jnp.arange(points, dtype=jnp.int32)
    phase_idx = longitude[:, None] * wavenums[None, :] % points
    angles = phase_idx.astype(jnp.float32) * (2.0 * math.pi / points)
    norm_scale = math.sqrt(2.0 / points)
    return (jnp.stack([jnp.cos(angles), -jnp.sin(angles)], axis=2) * norm_scale).astype(jnp.bfloat16)

def legendre_table(orders, lat_count, degrees):
    colatitude = (jnp.arange(lat_count, dtype=jnp.float32) + 0.5) * (math.pi / lat_count)
    cosine = jnp.cos(colatitude)
    sine_val = jnp.sin(colatitude)
    log_start = 0.5 * jnp.log((2.0 * orders + 1.0) / (4.0 * math.pi)) + 0.5 * (lax.lgamma(2.0 * orders + 1.0) - 2.0 * lax.lgamma(orders + 1.0) - orders * math.log(4.0))
    start_val = jnp.exp(log_start[:, None] + orders[:, None] * jnp.log(sine_val)[None, :])
    quad_weight = math.pi * jnp.sqrt(2.0 * sine_val / lat_count)
    order_col = orders[:, None]

    def advance(carried, degree):
        prev_one, before = carried
        level = degree.astype(jnp.float32)
        is_live = level > order_col
        beyond = level > order_col + 1.0
        lead_coef = jnp.where(is_live, jnp.sqrt(jnp.maximum(4.0 * level * level - 1.0, 0.0) / jnp.where(is_live, level * level - order_col * order_col, 1.0)), 0.0)
        back_num = jnp.maximum((level - 1.0) * (level - 1.0) - order_col * order_col, 0.0)
        back_coef = jnp.where(beyond, jnp.sqrt(back_num / jnp.where(beyond, 4.0 * (level - 1.0) * (level - 1.0) - 1.0, 1.0)), 0.0)
        newest = lead_coef * (cosine[None, :] * prev_one - back_coef * before) + jnp.where(level == order_col, start_val, 0.0)
        return ((newest, prev_one), newest)
    zeros_init = jnp.zeros((orders.shape[0], lat_count), jnp.float32)
    stacked = lax.scan(advance, (zeros_init, zeros_init), jnp.arange(degrees, dtype=jnp.int32))[1]
    return jnp.transpose(stacked, (1, 0, 2)) * quad_weight[None, None, :]

def gelu_slope(values):
    return 0.5 * (1.0 + lax.erf(values * 0.7071067811865476)) + values * jnp.exp(-0.5 * values * values) * 0.3989422804014327

def complex_product(left_re, left_im, right_re, right_im):
    return (left_re * right_re - left_im * right_im, left_re * right_im + left_im * right_re)

def through_bf16(values):
    return lax.optimization_barrier(values.astype(jnp.bfloat16)).astype(jnp.float32)

def reference(samples, cotangent, wave_owner, filter_weight, zonal_gain):
    slot_of, order_of = slot_tables(wave_owner, LAT_DEV, N_SPACE)
    wavenums = jnp.arange(MODES, dtype=jnp.int32)
    table = lax.optimization_barrier(fourier_table(wavenums, NLON)).astype(jnp.float32)
    legendre = through_bf16(legendre_table(wavenums.astype(jnp.float32), NLAT, MODES))
    gain_m = jnp.take(zonal_gain, slot_of, axis=1).astype(jnp.float32)
    grid = samples.astype(jnp.float32)
    weight_re = filter_weight[0].astype(jnp.float32)
    weight_im = filter_weight[1].astype(jnp.float32)

    def spectral_of(wavenum):
        table_col = lax.dynamic_index_in_dim(table, wavenum, 1, keepdims=False)
        fourier = through_bf16(jnp.einsum('bjkc,kr->bjrc', grid, table_col))
        legendre_m = lax.dynamic_index_in_dim(legendre, wavenum, 0, keepdims=False)
        spectral = jnp.einsum('lj,bjrc->blrc', legendre_m, fourier)
        gain_re = lax.dynamic_index_in_dim(gain_m[0], wavenum, 0, keepdims=False)
        gain_im = lax.dynamic_index_in_dim(gain_m[1], wavenum, 0, keepdims=False)
        kern_re, kern_im = complex_product(weight_re, weight_im, gain_re[None, :], gain_im[None, :])
        return (table_col, legendre_m, spectral, gain_re, gain_im, kern_re, kern_im)

    def forward_order(wavenum):
        table_col, legendre_m, spectral, gain_re, gain_im, kern_re, kern_im = spectral_of(wavenum)
        filt_re, filt_im = complex_product(spectral[:, :, 0], spectral[:, :, 1], kern_re[None], kern_im[None])
        filtered = through_bf16(jnp.stack([filt_re, filt_im], axis=2))
        return jnp.einsum('lj,blrc->bjrc', legendre_m, filtered).astype(jnp.bfloat16)
    zonal = lax.map(forward_order, wavenums)
    field = jnp.einsum('sbjrc,ksr->bjkc', zonal.astype(jnp.float32), table)
    dfield = through_bf16(cotangent.astype(jnp.float32) * gelu_slope(field))

    def backward_order(carried, wavenum):
        table_col, legendre_m, spectral, gain_re, gain_im, kern_re, kern_im = spectral_of(wavenum)
        dzonal = through_bf16(jnp.einsum('bjkc,kr->bjrc', dfield, table_col))
        dfiltered = jnp.einsum('lj,bjrc->blrc', legendre_m, dzonal)
        grad_re = dfiltered[:, :, 0]
        grad_im = dfiltered[:, :, 1]
        spec_re = spectral[:, :, 0]
        spec_im = spectral[:, :, 1]
        prod_re, prod_im = complex_product(spec_re, spec_im, gain_re[None, None, :], gain_im[None, None, :])
        wgrad = jnp.stack([lax.optimization_barrier(jnp.sum(grad_re * prod_re + grad_im * prod_im, axis=0)), lax.optimization_barrier(jnp.sum(grad_im * prod_re - grad_re * prod_im, axis=0))])
        other_re, other_im = complex_product(spec_re, spec_im, weight_re[None], weight_im[None])
        ggrad = jnp.stack([lax.optimization_barrier(jnp.sum(grad_re * other_re + grad_im * other_im, axis=(0, 1))), lax.optimization_barrier(jnp.sum(grad_im * other_re - grad_re * other_im, axis=(0, 1)))])
        dspec = through_bf16(jnp.stack([grad_re * kern_re[None] + grad_im * kern_im[None], grad_im * kern_re[None] - grad_re * kern_im[None]], axis=2))
        dfourier = jnp.einsum('lj,blrc->bjrc', legendre_m, dspec).astype(jnp.bfloat16)
        return (carried + wgrad, (ggrad, dfourier))
    weight_sum, (gain_rows, dfourier) = lax.scan(backward_order, jnp.zeros((2, MODES, C), jnp.float32), wavenums)
    sample_grad = (cotangent.astype(jnp.float32) + jnp.einsum('sbjrc,ksr->bjkc', dfourier.astype(jnp.float32), table)).astype(jnp.bfloat16)
    gain_grad = jnp.transpose(jnp.take(gain_rows, order_of, axis=0), (1, 0, 2))
    return (sample_grad, weight_sum.astype(jnp.bfloat16), gain_grad)
```

```python
import functools
import math

import jax
import jax.numpy as jnp
import numpy as np
from jax import lax
from jax.experimental import pallas as pl
from jax.experimental.pallas import tpu as pltpu
from jax.sharding import PartitionSpec as P

LANES = 128
HALF = LANES // 2


def slot_tables(wave_owner, per_device, devices):
    is_owner = (wave_owner[:, None] == jnp.arange(devices, dtype=jnp.int32)[None, :]).astype(
        jnp.int32
    )
    owner_rank = jnp.sum((jnp.cumsum(is_owner, axis=0) - 1) * is_owner, axis=1)
    slot_of = wave_owner * per_device + owner_rank
    total_modes = wave_owner.shape[0]
    positions = jnp.arange(total_modes, dtype=jnp.int32)
    matches = (slot_of[None, :] == positions[:, None]).astype(jnp.int32)
    order_of = jnp.sum(matches * positions[None, :], axis=1)
    return (slot_of, order_of)


def fourier_table(wavenums, points):
    longitude = jnp.arange(points, dtype=jnp.int32)
    phase_idx = longitude[:, None] * wavenums[None, :] % points
    angles = phase_idx.astype(jnp.float32) * (2.0 * math.pi / points)
    norm_scale = math.sqrt(2.0 / points)
    return (jnp.stack([jnp.cos(angles), -jnp.sin(angles)], axis=2) * norm_scale).astype(
        jnp.bfloat16
    )


def legendre_table(orders, lat_count, degrees):
    colatitude = (jnp.arange(lat_count, dtype=jnp.float32) + 0.5) * (math.pi / lat_count)
    cosine = jnp.cos(colatitude)
    sine_val = jnp.sin(colatitude)
    log_start = 0.5 * jnp.log((2.0 * orders + 1.0) / (4.0 * math.pi)) + 0.5 * (
        lax.lgamma(2.0 * orders + 1.0) - 2.0 * lax.lgamma(orders + 1.0) - orders * math.log(4.0)
    )
    start_val = jnp.exp(log_start[:, None] + orders[:, None] * jnp.log(sine_val)[None, :])
    quad_weight = math.pi * jnp.sqrt(2.0 * sine_val / lat_count)
    order_col = orders[:, None]

    def advance(carried, degree):
        prev_one, before = carried
        level = degree.astype(jnp.float32)
        is_live = level > order_col
        beyond = level > order_col + 1.0
        lead_coef = jnp.where(
            is_live,
            jnp.sqrt(
                jnp.maximum(4.0 * level * level - 1.0, 0.0)
                / jnp.where(is_live, level * level - order_col * order_col, 1.0)
            ),
            0.0,
        )
        back_num = jnp.maximum((level - 1.0) * (level - 1.0) - order_col * order_col, 0.0)
        back_coef = jnp.where(
            beyond,
            jnp.sqrt(back_num / jnp.where(beyond, 4.0 * (level - 1.0) * (level - 1.0) - 1.0, 1.0)),
            0.0,
        )
        newest = lead_coef * (cosine[None, :] * prev_one - back_coef * before) + jnp.where(
            level == order_col, start_val, 0.0
        )
        return ((newest, prev_one), newest)

    zeros_init = jnp.zeros((orders.shape[0], lat_count), jnp.float32)
    stacked = lax.scan(
        advance, (zeros_init, zeros_init), jnp.arange(degrees, dtype=jnp.int32), unroll=16
    )[1]
    return jnp.transpose(stacked, (1, 0, 2)) * quad_weight[None, None, :]


def gelu_slope(values):
    return (
        0.5 * (1.0 + lax.erf(values * 0.7071067811865476))
        + values * jnp.exp(-0.5 * values * values) * 0.3989422804014327
    )


def complex_product(left_re, left_im, right_re, right_im):
    return (left_re * right_re - left_im * right_im, left_re * right_im + left_im * right_re)


def analysis(legendre, columns):
    return jnp.einsum("ilj,ijrc->ilrc", legendre, columns, preferred_element_type=jnp.float32)


def synthesis(legendre, spectra):
    return jnp.einsum("ilj,ilrc->ijrc", legendre, spectra, preferred_element_type=jnp.float32)


def general_body(samples, cotangent, wave_owner, filter_weight, zonal_gain):
    devices = lax.axis_size("space")
    own_index = lax.axis_index("space")
    per_device = zonal_gain.shape[1]
    total_modes = wave_owner.shape[0]
    points = samples.shape[2]
    slot_of, order_of = slot_tables(wave_owner, per_device, devices)
    mine = lax.dynamic_slice_in_dim(order_of, own_index * per_device, per_device)
    table = fourier_table(order_of, points)
    legendre = legendre_table(mine.astype(jnp.float32), total_modes, total_modes).astype(
        jnp.bfloat16
    )
    grid = samples[0]
    cot_grid = cotangent[0]
    weight_re = filter_weight[0].astype(jnp.float32)[None]
    weight_im = filter_weight[1].astype(jnp.float32)[None]
    gain_re = zonal_gain[0].astype(jnp.float32)[:, None, :]
    gain_im = zonal_gain[1].astype(jnp.float32)[:, None, :]
    kern_re, kern_im = complex_product(weight_re, weight_im, gain_re, gain_im)
    fourier = jnp.einsum("jkc,ksr->sjrc", grid, table, preferred_element_type=jnp.float32).astype(
        jnp.bfloat16
    )
    owned = lax.all_to_all(fourier, "space", split_axis=0, concat_axis=1, tiled=True)
    spectral = analysis(legendre, owned)
    spec_re = spectral[:, :, 0]
    spec_im = spectral[:, :, 1]
    filt_re, filt_im = complex_product(spec_re, spec_im, kern_re, kern_im)
    filtered = jnp.stack([filt_re, filt_im], axis=2).astype(jnp.bfloat16)
    zonal = synthesis(legendre, filtered).astype(jnp.bfloat16)
    banded = lax.all_to_all(zonal, "space", split_axis=1, concat_axis=0, tiled=True)
    field = jnp.einsum("sjrc,ksr->jkc", banded, table, preferred_element_type=jnp.float32)
    dfield = (cot_grid.astype(jnp.float32) * gelu_slope(field)).astype(jnp.bfloat16)
    dzonal = jnp.einsum("jkc,ksr->sjrc", dfield, table, preferred_element_type=jnp.float32).astype(
        jnp.bfloat16
    )
    grad_owned = lax.all_to_all(dzonal, "space", split_axis=0, concat_axis=1, tiled=True)
    dfiltered = analysis(legendre, grad_owned)
    grad_re = dfiltered[:, :, 0]
    grad_im = dfiltered[:, :, 1]
    prod_re, prod_im = complex_product(spec_re, spec_im, gain_re, gain_im)
    weight_part = jnp.stack(
        [
            jnp.sum(grad_re * prod_re + grad_im * prod_im, axis=0),
            jnp.sum(grad_im * prod_re - grad_re * prod_im, axis=0),
        ]
    )
    other_re, other_im = complex_product(spec_re, spec_im, weight_re, weight_im)
    gain_part = jnp.stack(
        [
            jnp.sum(grad_re * other_re + grad_im * other_im, axis=1),
            jnp.sum(grad_im * other_re - grad_re * other_im, axis=1),
        ]
    )
    dspec = jnp.stack(
        [grad_re * kern_re + grad_im * kern_im, grad_im * kern_re - grad_re * kern_im], axis=2
    ).astype(jnp.bfloat16)
    dfourier = synthesis(legendre, dspec).astype(jnp.bfloat16)
    grad_banded = lax.all_to_all(dfourier, "space", split_axis=1, concat_axis=0, tiled=True)
    sample_grad = (
        cot_grid.astype(jnp.float32)
        + jnp.einsum("sjrc,ksr->jkc", grad_banded, table, preferred_element_type=jnp.float32)
    ).astype(jnp.bfloat16)
    weight_grad = lax.psum(weight_part, ("dp", "space")).astype(jnp.bfloat16)
    gain_grad = lax.psum(gain_part, "dp")
    return (sample_grad[None], weight_grad, gain_grad)


def host_tables(lats, points, modes):
    m = np.arange(modes, dtype=np.float64)
    angles = (np.arange(points)[:, None] * np.arange(modes)[None, :] % points) * (
        2.0 * math.pi / points
    )
    fourier = np.stack([np.cos(angles), -np.sin(angles)]) * math.sqrt(2.0 / points)
    fourier = fourier.astype(np.float32).astype(jnp.bfloat16).astype(np.float64)
    colat = (np.arange(lats) + 0.5) * (math.pi / lats)
    cosine, sine = np.cos(colat), np.sin(colat)
    log_start = np.array(
        [
            0.5 * math.log((2 * o + 1) / (4 * math.pi))
            + 0.5 * (math.lgamma(2 * o + 1) - 2 * math.lgamma(o + 1) - o * math.log(4.0))
            for o in range(modes)
        ]
    )
    pbar = np.zeros((modes, modes, lats))
    for o in range(modes):
        pbar[o, o] = np.exp(log_start[o] + m[o] * np.log(sine))
        for l in range(o + 1, modes):
            lead = math.sqrt((4 * l * l - 1) / (l * l - o * o))
            pbar[o, l] = lead * cosine * pbar[o, l - 1]
            if l > o + 1:
                back = math.sqrt(((l - 1) ** 2 - o * o) / (4 * (l - 1) ** 2 - 1))
                pbar[o, l] -= lead * back * pbar[o, l - 2]
    legendre = pbar * (math.pi * np.sqrt(2.0 * sine / lats))[None, None, :]
    legendre = legendre.astype(np.float32).astype(jnp.bfloat16).astype(np.float64)
    table = np.einsum("mlj,rkm->rmljk", legendre, fourier)
    table = table.reshape(2, modes, modes, lats // 2, 2, points).transpose(0, 1, 2, 4, 3, 5)
    table = table.reshape(2 * modes * modes, lats * points).astype(np.float32)
    return (table.astype(jnp.bfloat16), np.ascontiguousarray(table.T).astype(jnp.bfloat16))


def low(values):
    return values[:, :HALF]


def high(values):
    return values[:, HALF:]


def side(left, right):
    return jnp.concatenate([left, right], axis=1)


def stack_halves(values):
    return jnp.concatenate([low(values), high(values)], axis=0)


def whole_kernel(
    n,
    x_ref,
    cot_ref,
    owner_ref,
    weight_ref,
    gain_ref,
    table_hbm,
    turned_hbm,
    out_ref,
    wgrad_ref,
    ggrad_ref,
    table,
    turned,
    x_out,
    x_in,
    cot_out,
    cot_in,
    g_out,
    g_in,
    y_out,
    y_in,
    part_out,
    part_in,
    w_out,
    w_in,
    q_out,
    q_in,
    send_sem,
    recv_sem,
    pair_sem,
    load_sem,
):
    f32, bf16 = jnp.float32, jnp.bfloat16
    me = lax.axis_index("space")
    dp = lax.axis_index("dp")
    points = x_ref.shape[1]
    modes = weight_ref.shape[1]
    peers = [lax.rem(me + i, n) for i in range(n)]
    order = list(range(1, n))

    loads = [
        pltpu.make_async_copy(table_hbm, table, load_sem.at[0]),
        pltpu.make_async_copy(turned_hbm, turned, load_sem.at[1]),
    ]
    for load in loads:
        load.start()
    barrier = pltpu.get_barrier_semaphore()
    for i in order:
        pl.semaphore_signal(
            barrier, inc=1, device_id={"space": peers[i]}, device_id_type=pl.DeviceIdType.MESH
        )
    pl.semaphore_signal(
        barrier, inc=1, device_id={"dp": 1 - dp}, device_id_type=pl.DeviceIdType.MESH
    )

    def exchange(kind, source, target):
        copies = []
        for i in order:
            copies.append(
                pltpu.make_async_remote_copy(
                    src_ref=source.at[peers[i]],
                    dst_ref=target.at[me],
                    send_sem=send_sem.at[kind, i],
                    recv_sem=recv_sem.at[kind, i],
                    device_id={"space": peers[i]},
                    device_id_type=pl.DeviceIdType.MESH,
                )
            )
        for copy in copies:
            copy.start()
        target[me] = source[me]
        return copies

    def split(ref, out):
        first, second = ref[0], ref[1]
        for t in range(n // 2):
            a = first[:, t * LANES : (t + 1) * LANES]
            b = second[:, t * LANES : (t + 1) * LANES]
            out[2 * t] = side(low(a), low(b))
            out[2 * t + 1] = side(high(a), high(b))

    split(x_ref, x_out)
    for part in range(2):
        rows = gain_ref[part].astype(f32)
        for i in range(n):
            c = i * HALF
            g_out[i, part : part + 1, :] = side(
                rows[0:1, c : c + HALF], rows[1:2, c : c + HALF]
            )
    pl.semaphore_wait(barrier, n)
    copies = exchange(0, x_out, x_in)
    g_copies = exchange(1, g_out, g_in)
    split(cot_ref, cot_out)
    cot_copies = exchange(2, cot_out, cot_in)

    sub = lax.broadcasted_iota(jnp.int32, (modes, modes), 0)
    lane = lax.broadcasted_iota(jnp.int32, (modes, modes), 1)
    owner_row = jnp.broadcast_to(owner_ref[...], (modes, modes))
    owner_col = jnp.sum(jnp.where(sub == lane, owner_row, 0), axis=1, keepdims=True)
    same = jnp.where((owner_row == owner_col) & (lane < sub), 1, 0)
    slot = owner_col * 2 + jnp.sum(same, axis=1, keepdims=True)
    slot = jnp.broadcast_to(slot, (modes, LANES))
    odd = (lax.broadcasted_iota(jnp.int32, (modes, LANES), 1) >= HALF).astype(jnp.int32)
    masks = [slot == 2 * i + odd for i in range(n)]

    tile = pl.ds(pl.multiple_of((me // 2) * LANES, LANES), LANES)
    parity = lax.rem(me, 2)

    def my_weight(part):
        both = weight_ref[part, :, tile].astype(f32)
        return jnp.where(parity == 1, high(both), low(both))

    w_re, w_im = my_weight(0)[None], my_weight(1)[None]

    for copy in g_copies:
        copy.wait_recv()

    def my_gain(part):
        total = jnp.zeros((modes, LANES), f32)
        for i in range(n):
            row = jnp.broadcast_to(g_in[i, part : part + 1, :], (modes, LANES))
            total = total + jnp.where(masks[i], row, 0.0)
        return (low(total) + high(total))[:, None, :]

    g_re, g_im = my_gain(0), my_gain(1)
    k_re, k_im = complex_product(w_re, w_im, g_re, g_im)

    def dot(a, b):
        return jnp.dot(a, b, preferred_element_type=f32)

    def apart(values):
        cube = values.reshape(2, modes, modes, HALF)
        return (cube[0], cube[1])

    def joined(re, im):
        rows = modes * modes
        return jnp.concatenate(
            [re.astype(bf16).reshape(rows, HALF), im.astype(bf16).reshape(rows, HALF)], axis=0
        )

    for load in loads:
        load.wait()
    for copy in copies:
        copy.wait_recv()
    grid = stack_halves(x_in[...].reshape(n * points, LANES))
    s_re, s_im = apart(dot(table[...], grid))
    f_re, f_im = complex_product(s_re, s_im, k_re, k_im)
    field = dot(turned[...], joined(f_re, f_im))
    field = side(field[: n * points], field[n * points :])
    slope = gelu_slope(field)
    for copy in cot_copies:
        copy.wait_recv()
    cot = cot_in[...].reshape(n * points, LANES).astype(f32)
    dfield = stack_halves((cot * slope).astype(bf16))
    d_re, d_im = apart(dot(table[...], dfield))

    h_re = d_re * s_re + d_im * s_im
    h_im = d_im * s_re - d_re * s_im
    wg_re = jnp.sum(h_re * g_re + h_im * g_im, axis=0)
    wg_im = jnp.sum(h_im * g_re - h_re * g_im, axis=0)
    gg_re = jnp.sum(h_re * w_re + h_im * w_im, axis=1)
    gg_im = jnp.sum(h_im * w_re - h_re * w_im, axis=1)
    part_out[0] = side(wg_re, wg_im)
    part_out[1] = side(gg_re, gg_im)
    swap = pltpu.make_async_remote_copy(
        src_ref=part_out,
        dst_ref=part_in,
        send_sem=pair_sem.at[0],
        recv_sem=pair_sem.at[1],
        device_id={"dp": 1 - dp},
        device_id_type=pl.DeviceIdType.MESH,
    )
    swap.start()

    e_re = d_re * k_re + d_im * k_im
    e_im = d_im * k_re - d_re * k_im
    dgrid = dot(turned[...], joined(e_re, e_im))
    dgrid = side(dgrid[: n * points], dgrid[n * points :])
    y_out[...] = (cot + dgrid).astype(bf16).reshape(n, points, LANES)
    y_copies = exchange(3, y_out, y_in)

    swap.wait_recv()
    both_w = (part_out[0] + part_in[0]).astype(bf16)
    both_g = part_out[1] + part_in[1]
    w_out[...] = both_w
    w_copies = []
    for i in order:
        w_copies.append(
            pltpu.make_async_remote_copy(
                src_ref=w_out,
                dst_ref=w_in.at[me],
                send_sem=send_sem.at[4, i],
                recv_sem=recv_sem.at[4, i],
                device_id={"space": peers[i]},
                device_id_type=pl.DeviceIdType.MESH,
            )
        )
    for copy in w_copies:
        copy.start()
    w_in[me] = both_w
    twice = [side(low(both_g), low(both_g)), side(high(both_g), high(both_g))]
    for i in range(n):
        for part in range(2):
            q_out[i, part : part + 1, :] = jnp.sum(
                jnp.where(masks[i], twice[part], 0.0), axis=0, keepdims=True
            )
    q_copies = exchange(5, q_out, q_in)

    for copy in y_copies:
        copy.wait_recv()
    for t in range(n // 2):
        a, b = y_in[2 * t], y_in[2 * t + 1]
        columns = pl.ds(t * LANES, LANES)
        out_ref[0, :, columns] = side(low(a), low(b))
        out_ref[1, :, columns] = side(high(a), high(b))
    for copy in w_copies:
        copy.wait_recv()
    for t in range(n // 2):
        a, b = w_in[2 * t], w_in[2 * t + 1]
        columns = pl.ds(t * LANES, LANES)
        wgrad_ref[0, :, columns] = side(low(a), low(b))
        wgrad_ref[1, :, columns] = side(high(a), high(b))
    for copy in q_copies:
        copy.wait_recv()
    for t in range(n // 2):
        a, b = q_in[2 * t], q_in[2 * t + 1]
        columns = pl.ds(t * LANES, LANES)
        first, second = side(low(a), low(b)), side(high(a), high(b))
        for part in range(2):
            ggrad_ref[part, 0:1, columns] = first[part : part + 1]
            ggrad_ref[part, 1:2, columns] = second[part : part + 1]
    swap.wait_send()
    for group in (copies, g_copies, cot_copies, y_copies, w_copies, q_copies):
        for copy in group:
            copy.wait_send()


def channel_body(n, samples, cotangent, wave_owner, filter_weight, zonal_gain):
    lat_dev, points, channels = samples.shape[1:]
    modes = wave_owner.shape[0]
    table, turned = host_tables(lat_dev * n, points, modes)
    bf16, f32 = jnp.bfloat16, jnp.float32
    vmem = pl.BlockSpec(memory_space=pltpu.VMEM)
    hbm = pl.BlockSpec(memory_space=pl.ANY)
    block = pltpu.VMEM((n, points, LANES), bf16)
    small = pltpu.VMEM((n, 2, LANES), f32)
    out, wgrad, ggrad = pl.pallas_call(
        functools.partial(whole_kernel, n),
        out_shape=(
            jax.ShapeDtypeStruct((lat_dev, points, channels), bf16),
            jax.ShapeDtypeStruct((2, modes, channels), bf16),
            jax.ShapeDtypeStruct((2, zonal_gain.shape[1], channels), f32),
        ),
        in_specs=[vmem] * 5 + [hbm] * 2,
        out_specs=(vmem, vmem, vmem),
        scratch_shapes=[
            pltpu.VMEM(table.shape, bf16),
            pltpu.VMEM(turned.shape, bf16),
            block,
            block,
            block,
            block,
            small,
            small,
            block,
            block,
            pltpu.VMEM((2, modes, LANES), f32),
            pltpu.VMEM((2, modes, LANES), f32),
            pltpu.VMEM((modes, LANES), bf16),
            pltpu.VMEM((n, modes, LANES), bf16),
            small,
            small,
            pltpu.SemaphoreType.DMA((6, n)),
            pltpu.SemaphoreType.DMA((6, n)),
            pltpu.SemaphoreType.DMA((2,)),
            pltpu.SemaphoreType.DMA((2,)),
        ],
        compiler_params=pltpu.CompilerParams(
            collective_id=0, has_side_effects=True, vmem_limit_bytes=24 * 1024 * 1024
        ),
    )(
        samples[0],
        cotangent[0],
        wave_owner[None],
        filter_weight,
        zonal_gain,
        jnp.asarray(table),
        jnp.asarray(turned),
    )
    return (out[None], wgrad, ggrad)


def body(samples, cotangent, wave_owner, filter_weight, zonal_gain):
    devices = lax.axis_size("space")
    lat_dev, points, channels = samples.shape[1:]
    modes = wave_owner.shape[0]
    fits = (
        lax.axis_size("dp") == 2
        and samples.shape[0] == 1
        and lat_dev == 2
        and zonal_gain.shape[1] == 2
        and channels == devices * HALF
        and devices % 2 == 0
        and modes % 16 == 0
        and points % 16 == 0
        and modes * modes * devices * points * 16 <= 8 * 1024 * 1024
    )
    if fits:
        return channel_body(devices, samples, cotangent, wave_owner, filter_weight, zonal_gain)
    return general_body(samples, cotangent, wave_owner, filter_weight, zonal_gain)


def solution(mesh):
    in_specs = (
        P(("groups", "dp"), "space", None, None),
        P(("groups", "dp"), "space", None, None),
        P(),
        P(),
        P(None, "space", None),
    )
    out_specs = (
        P(("groups", "dp"), "space", None, None),
        P("groups", None, None),
        P("groups", "space", None),
    )
    return jax.shard_map(body, mesh=mesh, in_specs=in_specs, out_specs=out_specs, check_vma=False)
```

```python
import functools
import math

import jax
import jax.numpy as jnp
import numpy as np
from jax import lax
from jax.experimental import pallas as pl
from jax.experimental.pallas import tpu as pltpu
from jax.sharding import PartitionSpec as P

LANES = 128
HALF = LANES // 2


def slot_tables(wave_owner, per_device, devices):
    is_owner = (wave_owner[:, None] == jnp.arange(devices, dtype=jnp.int32)[None, :]).astype(
        jnp.int32
    )
    owner_rank = jnp.sum((jnp.cumsum(is_owner, axis=0) - 1) * is_owner, axis=1)
    slot_of = wave_owner * per_device + owner_rank
    total_modes = wave_owner.shape[0]
    positions = jnp.arange(total_modes, dtype=jnp.int32)
    matches = (slot_of[None, :] == positions[:, None]).astype(jnp.int32)
    order_of = jnp.sum(matches * positions[None, :], axis=1)
    return (slot_of, order_of)


def fourier_table(wavenums, points):
    longitude = jnp.arange(points, dtype=jnp.int32)
    phase_idx = longitude[:, None] * wavenums[None, :] % points
    angles = phase_idx.astype(jnp.float32) * (2.0 * math.pi / points)
    norm_scale = math.sqrt(2.0 / points)
    return (jnp.stack([jnp.cos(angles), -jnp.sin(angles)], axis=2) * norm_scale).astype(
        jnp.bfloat16
    )


def legendre_table(orders, lat_count, degrees):
    colatitude = (jnp.arange(lat_count, dtype=jnp.float32) + 0.5) * (math.pi / lat_count)
    cosine = jnp.cos(colatitude)
    sine_val = jnp.sin(colatitude)
    log_start = 0.5 * jnp.log((2.0 * orders + 1.0) / (4.0 * math.pi)) + 0.5 * (
        lax.lgamma(2.0 * orders + 1.0) - 2.0 * lax.lgamma(orders + 1.0) - orders * math.log(4.0)
    )
    start_val = jnp.exp(log_start[:, None] + orders[:, None] * jnp.log(sine_val)[None, :])
    quad_weight = math.pi * jnp.sqrt(2.0 * sine_val / lat_count)
    order_col = orders[:, None]

    def advance(carried, degree):
        prev_one, before = carried
        level = degree.astype(jnp.float32)
        is_live = level > order_col
        beyond = level > order_col + 1.0
        lead_coef = jnp.where(
            is_live,
            jnp.sqrt(
                jnp.maximum(4.0 * level * level - 1.0, 0.0)
                / jnp.where(is_live, level * level - order_col * order_col, 1.0)
            ),
            0.0,
        )
        back_num = jnp.maximum((level - 1.0) * (level - 1.0) - order_col * order_col, 0.0)
        back_coef = jnp.where(
            beyond,
            jnp.sqrt(back_num / jnp.where(beyond, 4.0 * (level - 1.0) * (level - 1.0) - 1.0, 1.0)),
            0.0,
        )
        newest = lead_coef * (cosine[None, :] * prev_one - back_coef * before) + jnp.where(
            level == order_col, start_val, 0.0
        )
        return ((newest, prev_one), newest)

    zeros_init = jnp.zeros((orders.shape[0], lat_count), jnp.float32)
    stacked = lax.scan(
        advance, (zeros_init, zeros_init), jnp.arange(degrees, dtype=jnp.int32), unroll=16
    )[1]
    return jnp.transpose(stacked, (1, 0, 2)) * quad_weight[None, None, :]


def gelu_slope(values):
    return (
        0.5 * (1.0 + lax.erf(values * 0.7071067811865476))
        + values * jnp.exp(-0.5 * values * values) * 0.3989422804014327
    )


def complex_product(left_re, left_im, right_re, right_im):
    return (left_re * right_re - left_im * right_im, left_re * right_im + left_im * right_re)


def analysis(legendre, columns):
    return jnp.einsum("ilj,ijrc->ilrc", legendre, columns, preferred_element_type=jnp.float32)


def synthesis(legendre, spectra):
    return jnp.einsum("ilj,ilrc->ijrc", legendre, spectra, preferred_element_type=jnp.float32)


def general_body(samples, cotangent, wave_owner, filter_weight, zonal_gain):
    devices = lax.axis_size("space")
    own_index = lax.axis_index("space")
    per_device = zonal_gain.shape[1]
    total_modes = wave_owner.shape[0]
    points = samples.shape[2]
    slot_of, order_of = slot_tables(wave_owner, per_device, devices)
    mine = lax.dynamic_slice_in_dim(order_of, own_index * per_device, per_device)
    table = fourier_table(order_of, points)
    legendre = legendre_table(mine.astype(jnp.float32), total_modes, total_modes).astype(
        jnp.bfloat16
    )
    grid = samples[0]
    cot_grid = cotangent[0]
    weight_re = filter_weight[0].astype(jnp.float32)[None]
    weight_im = filter_weight[1].astype(jnp.float32)[None]
    gain_re = zonal_gain[0].astype(jnp.float32)[:, None, :]
    gain_im = zonal_gain[1].astype(jnp.float32)[:, None, :]
    kern_re, kern_im = complex_product(weight_re, weight_im, gain_re, gain_im)
    fourier = jnp.einsum("jkc,ksr->sjrc", grid, table, preferred_element_type=jnp.float32).astype(
        jnp.bfloat16
    )
    owned = lax.all_to_all(fourier, "space", split_axis=0, concat_axis=1, tiled=True)
    spectral = analysis(legendre, owned)
    spec_re = spectral[:, :, 0]
    spec_im = spectral[:, :, 1]
    filt_re, filt_im = complex_product(spec_re, spec_im, kern_re, kern_im)
    filtered = jnp.stack([filt_re, filt_im], axis=2).astype(jnp.bfloat16)
    zonal = synthesis(legendre, filtered).astype(jnp.bfloat16)
    banded = lax.all_to_all(zonal, "space", split_axis=1, concat_axis=0, tiled=True)
    field = jnp.einsum("sjrc,ksr->jkc", banded, table, preferred_element_type=jnp.float32)
    dfield = (cot_grid.astype(jnp.float32) * gelu_slope(field)).astype(jnp.bfloat16)
    dzonal = jnp.einsum("jkc,ksr->sjrc", dfield, table, preferred_element_type=jnp.float32).astype(
        jnp.bfloat16
    )
    grad_owned = lax.all_to_all(dzonal, "space", split_axis=0, concat_axis=1, tiled=True)
    dfiltered = analysis(legendre, grad_owned)
    grad_re = dfiltered[:, :, 0]
    grad_im = dfiltered[:, :, 1]
    prod_re, prod_im = complex_product(spec_re, spec_im, gain_re, gain_im)
    weight_part = jnp.stack(
        [
            jnp.sum(grad_re * prod_re + grad_im * prod_im, axis=0),
            jnp.sum(grad_im * prod_re - grad_re * prod_im, axis=0),
        ]
    )
    other_re, other_im = complex_product(spec_re, spec_im, weight_re, weight_im)
    gain_part = jnp.stack(
        [
            jnp.sum(grad_re * other_re + grad_im * other_im, axis=1),
            jnp.sum(grad_im * other_re - grad_re * other_im, axis=1),
        ]
    )
    dspec = jnp.stack(
        [grad_re * kern_re + grad_im * kern_im, grad_im * kern_re - grad_re * kern_im], axis=2
    ).astype(jnp.bfloat16)
    dfourier = synthesis(legendre, dspec).astype(jnp.bfloat16)
    grad_banded = lax.all_to_all(dfourier, "space", split_axis=1, concat_axis=0, tiled=True)
    sample_grad = (
        cot_grid.astype(jnp.float32)
        + jnp.einsum("sjrc,ksr->jkc", grad_banded, table, preferred_element_type=jnp.float32)
    ).astype(jnp.bfloat16)
    weight_grad = lax.psum(weight_part, ("dp", "space")).astype(jnp.bfloat16)
    gain_grad = lax.psum(gain_part, "dp")
    return (sample_grad[None], weight_grad, gain_grad)


def host_tables(lats, points, modes):
    m = np.arange(modes, dtype=np.float64)
    angles = (np.arange(points)[:, None] * np.arange(modes)[None, :] % points) * (
        2.0 * math.pi / points
    )
    fourier = np.stack([np.cos(angles), -np.sin(angles)]) * math.sqrt(2.0 / points)
    fourier = fourier.astype(np.float32).astype(jnp.bfloat16).astype(np.float64)
    colat = (np.arange(lats) + 0.5) * (math.pi / lats)
    cosine, sine = np.cos(colat), np.sin(colat)
    log_start = np.array(
        [
            0.5 * math.log((2 * o + 1) / (4 * math.pi))
            + 0.5 * (math.lgamma(2 * o + 1) - 2 * math.lgamma(o + 1) - o * math.log(4.0))
            for o in range(modes)
        ]
    )
    pbar = np.zeros((modes, modes, lats))
    for o in range(modes):
        pbar[o, o] = np.exp(log_start[o] + m[o] * np.log(sine))
        for l in range(o + 1, modes):
            lead = math.sqrt((4 * l * l - 1) / (l * l - o * o))
            pbar[o, l] = lead * cosine * pbar[o, l - 1]
            if l > o + 1:
                back = math.sqrt(((l - 1) ** 2 - o * o) / (4 * (l - 1) ** 2 - 1))
                pbar[o, l] -= lead * back * pbar[o, l - 2]
    legendre = pbar * (math.pi * np.sqrt(2.0 * sine / lats))[None, None, :]
    legendre = legendre.astype(np.float32).astype(jnp.bfloat16).astype(np.float64)
    table = np.einsum("mlj,rkm->rmljk", legendre, fourier)
    table = table.reshape(2, modes, modes, lats // 2, 2, points).transpose(0, 1, 2, 4, 3, 5)
    table = table.reshape(2 * modes * modes, lats * points).astype(np.float32)
    return (table.astype(jnp.bfloat16), np.ascontiguousarray(table.T).astype(jnp.bfloat16))


def low(values):
    return values[:, :HALF]


def high(values):
    return values[:, HALF:]


def side(left, right):
    return jnp.concatenate([left, right], axis=1)


def stack_halves(values):
    return jnp.concatenate([low(values), high(values)], axis=0)


def whole_kernel(
    n,
    x_hbm,
    cot_hbm,
    owner_hbm,
    weight_hbm,
    gain_hbm,
    table_hbm,
    turned_hbm,
    y_in,
    w_in,
    q_in,
    x_ref,
    cot_ref,
    owner_ref,
    weight_ref,
    gain_ref,
    table,
    turned,
    x_out,
    x_in,
    cot_out,
    cot_in,
    g_out,
    g_in,
    y_out,
    part_out,
    part_in,
    w_out,
    q_out,
    send_sem,
    recv_sem,
    pair_sem,
    load_sem,
):
    f32, bf16 = jnp.float32, jnp.bfloat16
    me = lax.axis_index("space")
    dp = lax.axis_index("dp")
    points = x_ref.shape[1]
    modes = weight_ref.shape[1]
    peers = [lax.rem(me + i, n) for i in range(n)]
    order = list(range(1, n))

    loads = [
        pltpu.make_async_copy(source, target, load_sem.at[i])
        for i, (source, target) in enumerate(
            [
                (x_hbm, x_ref),
                (gain_hbm, gain_ref),
                (cot_hbm, cot_ref),
                (owner_hbm, owner_ref),
                (weight_hbm, weight_ref),
                (table_hbm, table),
                (turned_hbm, turned),
            ]
        )
    ]
    for load in loads:
        load.start()
    barrier = pltpu.get_barrier_semaphore()
    for i in order:
        pl.semaphore_signal(
            barrier, inc=1, device_id={"space": peers[i]}, device_id_type=pl.DeviceIdType.MESH
        )
    pl.semaphore_signal(
        barrier, inc=1, device_id={"dp": 1 - dp}, device_id_type=pl.DeviceIdType.MESH
    )

    def exchange(kind, source, target):
        copies = []
        for i in order:
            copies.append(
                pltpu.make_async_remote_copy(
                    src_ref=source.at[peers[i]],
                    dst_ref=target.at[me],
                    send_sem=send_sem.at[kind, i],
                    recv_sem=recv_sem.at[kind, i],
                    device_id={"space": peers[i]},
                    device_id_type=pl.DeviceIdType.MESH,
                )
            )
        for copy in copies:
            copy.start()
        target[me] = source[me]
        return copies

    def split(ref, out):
        first, second = ref[0], ref[1]
        for t in range(n // 2):
            a = first[:, t * LANES : (t + 1) * LANES]
            b = second[:, t * LANES : (t + 1) * LANES]
            out[2 * t] = side(low(a), low(b))
            out[2 * t + 1] = side(high(a), high(b))

    loads[0].wait()
    split(x_ref, x_out)
    loads[1].wait()
    for part in range(2):
        rows = gain_ref[part].astype(f32)
        for i in range(n):
            c = i * HALF
            g_out[i, part : part + 1, :] = side(
                rows[0:1, c : c + HALF], rows[1:2, c : c + HALF]
            )
    pl.semaphore_wait(barrier, n)
    copies = exchange(0, x_out, x_in)
    g_copies = exchange(1, g_out, g_in)
    loads[2].wait()
    split(cot_ref, cot_out)
    cot_copies = exchange(2, cot_out, cot_in)

    loads[3].wait()
    loads[4].wait()
    sub = lax.broadcasted_iota(jnp.int32, (modes, modes), 0)
    lane = lax.broadcasted_iota(jnp.int32, (modes, modes), 1)
    owner_row = jnp.broadcast_to(owner_ref[...], (modes, modes))
    owner_col = jnp.sum(jnp.where(sub == lane, owner_row, 0), axis=1, keepdims=True)
    same = jnp.where((owner_row == owner_col) & (lane < sub), 1, 0)
    slot = owner_col * 2 + jnp.sum(same, axis=1, keepdims=True)
    slot = jnp.broadcast_to(slot, (modes, LANES))
    odd = (lax.broadcasted_iota(jnp.int32, (modes, LANES), 1) >= HALF).astype(jnp.int32)
    masks = [slot == 2 * i + odd for i in range(n)]

    tile = pl.ds(pl.multiple_of((me // 2) * LANES, LANES), LANES)
    parity = lax.rem(me, 2)

    def my_weight(part):
        both = weight_ref[part, :, tile].astype(f32)
        return jnp.where(parity == 1, high(both), low(both))

    w_re, w_im = my_weight(0)[None], my_weight(1)[None]

    for copy in g_copies:
        copy.wait_recv()

    def my_gain(part):
        total = jnp.zeros((modes, LANES), f32)
        for i in range(n):
            row = jnp.broadcast_to(g_in[i, part : part + 1, :], (modes, LANES))
            total = total + jnp.where(masks[i], row, 0.0)
        return (low(total) + high(total))[:, None, :]

    g_re, g_im = my_gain(0), my_gain(1)
    k_re, k_im = complex_product(w_re, w_im, g_re, g_im)

    def dot(a, b):
        return jnp.dot(a, b, preferred_element_type=f32)

    def apart(values):
        cube = values.reshape(2, modes, modes, HALF)
        return (cube[0], cube[1])

    def joined(re, im):
        rows = modes * modes
        return jnp.concatenate(
            [re.astype(bf16).reshape(rows, HALF), im.astype(bf16).reshape(rows, HALF)], axis=0
        )

    loads[5].wait()
    loads[6].wait()
    for copy in copies:
        copy.wait_recv()
    grid = stack_halves(x_in[...].reshape(n * points, LANES))
    s_re, s_im = apart(dot(table[...], grid))
    f_re, f_im = complex_product(s_re, s_im, k_re, k_im)
    field = dot(turned[...], joined(f_re, f_im))
    field = side(field[: n * points], field[n * points :])
    slope = gelu_slope(field)
    for copy in cot_copies:
        copy.wait_recv()
    cot = cot_in[...].reshape(n * points, LANES).astype(f32)
    dfield = stack_halves((cot * slope).astype(bf16))
    d_re, d_im = apart(dot(table[...], dfield))

    h_re = d_re * s_re + d_im * s_im
    h_im = d_im * s_re - d_re * s_im
    wg_re = jnp.sum(h_re * g_re + h_im * g_im, axis=0)
    wg_im = jnp.sum(h_im * g_re - h_re * g_im, axis=0)
    gg_re = jnp.sum(h_re * w_re + h_im * w_im, axis=1)
    gg_im = jnp.sum(h_im * w_re - h_re * w_im, axis=1)
    part_out[0] = side(wg_re, wg_im)
    part_out[1] = side(gg_re, gg_im)
    swap = pltpu.make_async_remote_copy(
        src_ref=part_out,
        dst_ref=part_in,
        send_sem=pair_sem.at[0],
        recv_sem=pair_sem.at[1],
        device_id={"dp": 1 - dp},
        device_id_type=pl.DeviceIdType.MESH,
    )
    swap.start()

    e_re = d_re * k_re + d_im * k_im
    e_im = d_im * k_re - d_re * k_im
    dgrid = dot(turned[...], joined(e_re, e_im))
    dgrid = side(dgrid[: n * points], dgrid[n * points :])
    y_out[...] = (cot + dgrid).astype(bf16).reshape(n, points, LANES)
    y_copies = exchange(3, y_out, y_in)

    swap.wait_recv()
    both_w = (part_out[0] + part_in[0]).astype(bf16)
    both_g = part_out[1] + part_in[1]
    w_out[...] = both_w
    w_copies = []
    for i in order:
        w_copies.append(
            pltpu.make_async_remote_copy(
                src_ref=w_out,
                dst_ref=w_in.at[me],
                send_sem=send_sem.at[4, i],
                recv_sem=recv_sem.at[4, i],
                device_id={"space": peers[i]},
                device_id_type=pl.DeviceIdType.MESH,
            )
        )
    for copy in w_copies:
        copy.start()
    w_in[me] = both_w
    twice = [side(low(both_g), low(both_g)), side(high(both_g), high(both_g))]
    for i in range(n):
        for part in range(2):
            q_out[i, part : part + 1, :] = jnp.sum(
                jnp.where(masks[i], twice[part], 0.0), axis=0, keepdims=True
            )
    q_copies = exchange(5, q_out, q_in)

    for group in (y_copies, w_copies, q_copies):
        for copy in group:
            copy.wait_recv()
    swap.wait_send()
    for group in (copies, g_copies, cot_copies, y_copies, w_copies, q_copies):
        for copy in group:
            copy.wait_send()


def place_kernel(
    n, y_in, w_in, q_in, out_hbm, wgrad_hbm, ggrad_hbm, out_ref, wgrad_ref, ggrad_ref, sem
):
    for t in range(n // 2):
        columns = slice(t * LANES, (t + 1) * LANES)
        a, b = y_in[2 * t], y_in[2 * t + 1]
        out_ref[0, :, columns] = side(low(a), low(b))
        out_ref[1, :, columns] = side(high(a), high(b))
    stores = [pltpu.make_async_copy(out_ref, out_hbm, sem.at[0])]
    stores[0].start()
    for t in range(n // 2):
        columns = slice(t * LANES, (t + 1) * LANES)
        a, b = w_in[2 * t], w_in[2 * t + 1]
        wgrad_ref[0, :, columns] = side(low(a), low(b))
        wgrad_ref[1, :, columns] = side(high(a), high(b))
        a, b = q_in[2 * t], q_in[2 * t + 1]
        first, second = side(low(a), low(b)), side(high(a), high(b))
        for part in range(2):
            ggrad_ref[part, 0:1, columns] = first[part : part + 1]
            ggrad_ref[part, 1:2, columns] = second[part : part + 1]
    stores.append(pltpu.make_async_copy(wgrad_ref, wgrad_hbm, sem.at[1]))
    stores.append(pltpu.make_async_copy(ggrad_ref, ggrad_hbm, sem.at[2]))
    for store in stores[1:]:
        store.start()
    for store in stores:
        store.wait()


def channel_body(n, samples, cotangent, wave_owner, filter_weight, zonal_gain):
    lat_dev, points, channels = samples.shape[1:]
    modes = wave_owner.shape[0]
    table, turned = host_tables(lat_dev * n, points, modes)
    bf16, f32 = jnp.bfloat16, jnp.float32
    vmem = pl.BlockSpec(memory_space=pltpu.VMEM)
    hbm = pl.BlockSpec(memory_space=pltpu.HBM)
    block = pltpu.VMEM((n, points, LANES), bf16)
    small = pltpu.VMEM((n, 2, LANES), f32)
    pair = pltpu.VMEM((2, modes, LANES), f32)
    operands = (
        samples[0],
        cotangent[0],
        wave_owner[None],
        filter_weight,
        zonal_gain,
        jnp.asarray(table),
        jnp.asarray(turned),
    )
    operands = [pltpu.with_memory_space_constraint(x, pltpu.HBM) for x in operands]
    received = pl.pallas_call(
        functools.partial(whole_kernel, n),
        out_shape=(
            pltpu.VMEM((n, points, LANES), bf16),
            pltpu.VMEM((n, modes, LANES), bf16),
            pltpu.VMEM((n, 2, LANES), f32),
        ),
        in_specs=[hbm] * len(operands),
        out_specs=(vmem, vmem, vmem),
        scratch_shapes=[pltpu.VMEM(x.shape, x.dtype) for x in operands]
        + [
            block,
            block,
            block,
            block,
            small,
            small,
            block,
            pair,
            pair,
            pltpu.VMEM((modes, LANES), bf16),
            small,
            pltpu.SemaphoreType.DMA((6, n)),
            pltpu.SemaphoreType.DMA((6, n)),
            pltpu.SemaphoreType.DMA((2,)),
            pltpu.SemaphoreType.DMA((len(operands),)),
        ],
        compiler_params=pltpu.CompilerParams(
            collective_id=0, has_side_effects=True, vmem_limit_bytes=24 * 1024 * 1024
        ),
    )(*operands)
    results = (
        jax.ShapeDtypeStruct((lat_dev, points, channels), bf16),
        jax.ShapeDtypeStruct((2, modes, channels), bf16),
        jax.ShapeDtypeStruct((2, zonal_gain.shape[1], channels), f32),
    )
    out, wgrad, ggrad = pl.pallas_call(
        functools.partial(place_kernel, n),
        out_shape=results,
        in_specs=[vmem] * 3,
        out_specs=(hbm, hbm, hbm),
        scratch_shapes=[pltpu.VMEM(x.shape, x.dtype) for x in results]
        + [pltpu.SemaphoreType.DMA((3,))],
    )(*received)
    return (out[None], wgrad, ggrad)


def body(samples, cotangent, wave_owner, filter_weight, zonal_gain):
    devices = lax.axis_size("space")
    lat_dev, points, channels = samples.shape[1:]
    modes = wave_owner.shape[0]
    fits = (
        lax.axis_size("dp") == 2
        and samples.shape[0] == 1
        and lat_dev == 2
        and zonal_gain.shape[1] == 2
        and channels == devices * HALF
        and devices % 2 == 0
        and modes % 16 == 0
        and points % 16 == 0
        and modes * modes * devices * points * 16 <= 8 * 1024 * 1024
    )
    if fits:
        return channel_body(devices, samples, cotangent, wave_owner, filter_weight, zonal_gain)
    return general_body(samples, cotangent, wave_owner, filter_weight, zonal_gain)


def solution(mesh):
    in_specs = (
        P(("groups", "dp"), "space", None, None),
        P(("groups", "dp"), "space", None, None),
        P(),
        P(),
        P(None, "space", None),
    )
    out_specs = (
        P(("groups", "dp"), "space", None, None),
        P("groups", None, None),
        P("groups", "space", None),
    )
    return jax.shard_map(body, mesh=mesh, in_specs=in_specs, out_specs=out_specs, check_vma=False)
```

```python
import functools
import math

import jax
import jax.numpy as jnp
import numpy as np
from jax import lax
from jax.experimental import pallas as pl
from jax.experimental.pallas import tpu as pltpu
from jax.sharding import PartitionSpec as P

LANES = 128
HALF = LANES // 2


def slot_tables(wave_owner, per_device, devices):
    is_owner = (wave_owner[:, None] == jnp.arange(devices, dtype=jnp.int32)[None, :]).astype(
        jnp.int32
    )
    owner_rank = jnp.sum((jnp.cumsum(is_owner, axis=0) - 1) * is_owner, axis=1)
    slot_of = wave_owner * per_device + owner_rank
    total_modes = wave_owner.shape[0]
    positions = jnp.arange(total_modes, dtype=jnp.int32)
    matches = (slot_of[None, :] == positions[:, None]).astype(jnp.int32)
    order_of = jnp.sum(matches * positions[None, :], axis=1)
    return (slot_of, order_of)


def fourier_table(wavenums, points):
    longitude = jnp.arange(points, dtype=jnp.int32)
    phase_idx = longitude[:, None] * wavenums[None, :] % points
    angles = phase_idx.astype(jnp.float32) * (2.0 * math.pi / points)
    norm_scale = math.sqrt(2.0 / points)
    return (jnp.stack([jnp.cos(angles), -jnp.sin(angles)], axis=2) * norm_scale).astype(
        jnp.bfloat16
    )


def legendre_table(orders, lat_count, degrees):
    colatitude = (jnp.arange(lat_count, dtype=jnp.float32) + 0.5) * (math.pi / lat_count)
    cosine = jnp.cos(colatitude)
    sine_val = jnp.sin(colatitude)
    log_start = 0.5 * jnp.log((2.0 * orders + 1.0) / (4.0 * math.pi)) + 0.5 * (
        lax.lgamma(2.0 * orders + 1.0) - 2.0 * lax.lgamma(orders + 1.0) - orders * math.log(4.0)
    )
    start_val = jnp.exp(log_start[:, None] + orders[:, None] * jnp.log(sine_val)[None, :])
    quad_weight = math.pi * jnp.sqrt(2.0 * sine_val / lat_count)
    order_col = orders[:, None]

    def advance(carried, degree):
        prev_one, before = carried
        level = degree.astype(jnp.float32)
        is_live = level > order_col
        beyond = level > order_col + 1.0
        lead_coef = jnp.where(
            is_live,
            jnp.sqrt(
                jnp.maximum(4.0 * level * level - 1.0, 0.0)
                / jnp.where(is_live, level * level - order_col * order_col, 1.0)
            ),
            0.0,
        )
        back_num = jnp.maximum((level - 1.0) * (level - 1.0) - order_col * order_col, 0.0)
        back_coef = jnp.where(
            beyond,
            jnp.sqrt(back_num / jnp.where(beyond, 4.0 * (level - 1.0) * (level - 1.0) - 1.0, 1.0)),
            0.0,
        )
        newest = lead_coef * (cosine[None, :] * prev_one - back_coef * before) + jnp.where(
            level == order_col, start_val, 0.0
        )
        return ((newest, prev_one), newest)

    zeros_init = jnp.zeros((orders.shape[0], lat_count), jnp.float32)
    stacked = lax.scan(
        advance, (zeros_init, zeros_init), jnp.arange(degrees, dtype=jnp.int32), unroll=16
    )[1]
    return jnp.transpose(stacked, (1, 0, 2)) * quad_weight[None, None, :]


def gelu_slope(values):
    return (
        0.5 * (1.0 + lax.erf(values * 0.7071067811865476))
        + values * jnp.exp(-0.5 * values * values) * 0.3989422804014327
    )


def complex_product(left_re, left_im, right_re, right_im):
    return (left_re * right_re - left_im * right_im, left_re * right_im + left_im * right_re)


def analysis(legendre, columns):
    return jnp.einsum("ilj,ijrc->ilrc", legendre, columns, preferred_element_type=jnp.float32)


def synthesis(legendre, spectra):
    return jnp.einsum("ilj,ilrc->ijrc", legendre, spectra, preferred_element_type=jnp.float32)


def general_body(samples, cotangent, wave_owner, filter_weight, zonal_gain):
    devices = lax.axis_size("space")
    own_index = lax.axis_index("space")
    per_device = zonal_gain.shape[1]
    total_modes = wave_owner.shape[0]
    points = samples.shape[2]
    slot_of, order_of = slot_tables(wave_owner, per_device, devices)
    mine = lax.dynamic_slice_in_dim(order_of, own_index * per_device, per_device)
    table = fourier_table(order_of, points)
    legendre = legendre_table(mine.astype(jnp.float32), total_modes, total_modes).astype(
        jnp.bfloat16
    )
    grid = samples[0]
    cot_grid = cotangent[0]
    weight_re = filter_weight[0].astype(jnp.float32)[None]
    weight_im = filter_weight[1].astype(jnp.float32)[None]
    gain_re = zonal_gain[0].astype(jnp.float32)[:, None, :]
    gain_im = zonal_gain[1].astype(jnp.float32)[:, None, :]
    kern_re, kern_im = complex_product(weight_re, weight_im, gain_re, gain_im)
    fourier = jnp.einsum("jkc,ksr->sjrc", grid, table, preferred_element_type=jnp.float32).astype(
        jnp.bfloat16
    )
    owned = lax.all_to_all(fourier, "space", split_axis=0, concat_axis=1, tiled=True)
    spectral = analysis(legendre, owned)
    spec_re = spectral[:, :, 0]
    spec_im = spectral[:, :, 1]
    filt_re, filt_im = complex_product(spec_re, spec_im, kern_re, kern_im)
    filtered = jnp.stack([filt_re, filt_im], axis=2).astype(jnp.bfloat16)
    zonal = synthesis(legendre, filtered).astype(jnp.bfloat16)
    banded = lax.all_to_all(zonal, "space", split_axis=1, concat_axis=0, tiled=True)
    field = jnp.einsum("sjrc,ksr->jkc", banded, table, preferred_element_type=jnp.float32)
    dfield = (cot_grid.astype(jnp.float32) * gelu_slope(field)).astype(jnp.bfloat16)
    dzonal = jnp.einsum("jkc,ksr->sjrc", dfield, table, preferred_element_type=jnp.float32).astype(
        jnp.bfloat16
    )
    grad_owned = lax.all_to_all(dzonal, "space", split_axis=0, concat_axis=1, tiled=True)
    dfiltered = analysis(legendre, grad_owned)
    grad_re = dfiltered[:, :, 0]
    grad_im = dfiltered[:, :, 1]
    prod_re, prod_im = complex_product(spec_re, spec_im, gain_re, gain_im)
    weight_part = jnp.stack(
        [
            jnp.sum(grad_re * prod_re + grad_im * prod_im, axis=0),
            jnp.sum(grad_im * prod_re - grad_re * prod_im, axis=0),
        ]
    )
    other_re, other_im = complex_product(spec_re, spec_im, weight_re, weight_im)
    gain_part = jnp.stack(
        [
            jnp.sum(grad_re * other_re + grad_im * other_im, axis=1),
            jnp.sum(grad_im * other_re - grad_re * other_im, axis=1),
        ]
    )
    dspec = jnp.stack(
        [grad_re * kern_re + grad_im * kern_im, grad_im * kern_re - grad_re * kern_im], axis=2
    ).astype(jnp.bfloat16)
    dfourier = synthesis(legendre, dspec).astype(jnp.bfloat16)
    grad_banded = lax.all_to_all(dfourier, "space", split_axis=1, concat_axis=0, tiled=True)
    sample_grad = (
        cot_grid.astype(jnp.float32)
        + jnp.einsum("sjrc,ksr->jkc", grad_banded, table, preferred_element_type=jnp.float32)
    ).astype(jnp.bfloat16)
    weight_grad = lax.psum(weight_part, ("dp", "space")).astype(jnp.bfloat16)
    gain_grad = lax.psum(gain_part, "dp")
    return (sample_grad[None], weight_grad, gain_grad)


def host_tables(lats, points, modes):
    m = np.arange(modes, dtype=np.float64)
    angles = (np.arange(points)[:, None] * np.arange(modes)[None, :] % points) * (
        2.0 * math.pi / points
    )
    fourier = np.stack([np.cos(angles), -np.sin(angles)]) * math.sqrt(2.0 / points)
    fourier = fourier.astype(np.float32).astype(jnp.bfloat16).astype(np.float64)
    colat = (np.arange(lats) + 0.5) * (math.pi / lats)
    cosine, sine = np.cos(colat), np.sin(colat)
    log_start = np.array(
        [
            0.5 * math.log((2 * o + 1) / (4 * math.pi))
            + 0.5 * (math.lgamma(2 * o + 1) - 2 * math.lgamma(o + 1) - o * math.log(4.0))
            for o in range(modes)
        ]
    )
    pbar = np.zeros((modes, modes, lats))
    for o in range(modes):
        pbar[o, o] = np.exp(log_start[o] + m[o] * np.log(sine))
        for l in range(o + 1, modes):
            lead = math.sqrt((4 * l * l - 1) / (l * l - o * o))
            pbar[o, l] = lead * cosine * pbar[o, l - 1]
            if l > o + 1:
                back = math.sqrt(((l - 1) ** 2 - o * o) / (4 * (l - 1) ** 2 - 1))
                pbar[o, l] -= lead * back * pbar[o, l - 2]
    legendre = pbar * (math.pi * np.sqrt(2.0 * sine / lats))[None, None, :]
    legendre = legendre.astype(np.float32).astype(jnp.bfloat16).astype(np.float64)
    table = np.einsum("mlj,rkm->rmljk", legendre, fourier)
    table = table.reshape(2, modes, modes, lats // 2, 2, points).transpose(0, 1, 2, 4, 3, 5)
    table = table.reshape(2 * modes * modes, lats * points).astype(np.float32)
    return (table.astype(jnp.bfloat16), np.ascontiguousarray(table.T).astype(jnp.bfloat16))


def low(values):
    return values[:, :HALF]


def high(values):
    return values[:, HALF:]


def side(left, right):
    return jnp.concatenate([left, right], axis=1)


def stack_halves(values):
    return jnp.concatenate([low(values), high(values)], axis=0)


def whole_kernel(
    n,
    x_hbm,
    cot_hbm,
    owner_hbm,
    weight_hbm,
    gain_hbm,
    table_hbm,
    turned_hbm,
    y_in,
    w_in,
    q_in,
    x_ref,
    cot_ref,
    owner_ref,
    weight_ref,
    gain_ref,
    table,
    turned,
    x_out,
    x_in,
    cot_out,
    cot_in,
    g_out,
    g_in,
    y_out,
    part_out,
    part_in,
    w_out,
    q_out,
    send_sem,
    recv_sem,
    pair_sem,
    load_sem,
):
    f32, bf16 = jnp.float32, jnp.bfloat16
    me = lax.axis_index("space")
    dp = lax.axis_index("dp")
    points = x_ref.shape[1]
    modes = weight_ref.shape[1]
    peers = [me ^ i for i in range(n)]
    order = list(range(n - 1, 0, -1))

    barrier = pltpu.get_barrier_semaphore()
    for i in order:
        pl.semaphore_signal(
            barrier, inc=1, device_id={"space": peers[i]}, device_id_type=pl.DeviceIdType.MESH
        )
    pl.semaphore_signal(
        barrier, inc=1, device_id={"dp": 1 - dp}, device_id_type=pl.DeviceIdType.MESH
    )
    loads = [
        pltpu.make_async_copy(source, target, load_sem.at[i])
        for i, (source, target) in enumerate(
            [
                (x_hbm, x_ref),
                (gain_hbm, gain_ref),
                (cot_hbm, cot_ref),
                (owner_hbm, owner_ref),
                (weight_hbm, weight_ref),
                (table_hbm, table),
                (turned_hbm, turned),
            ]
        )
    ]
    for load in loads:
        load.start()
    def exchange(kind, source, target):
        copies = []
        for i in order:
            copies.append(
                pltpu.make_async_remote_copy(
                    src_ref=source.at[peers[i]],
                    dst_ref=target.at[me],
                    send_sem=send_sem.at[kind, i],
                    recv_sem=recv_sem.at[kind, i],
                    device_id={"space": peers[i]},
                    device_id_type=pl.DeviceIdType.MESH,
                )
            )
        for copy in copies:
            copy.start()
        target[me] = source[me]
        return copies

    def split(ref, out):
        first, second = ref[0], ref[1]
        for t in range(n // 2):
            a = first[:, t * LANES : (t + 1) * LANES]
            b = second[:, t * LANES : (t + 1) * LANES]
            out[2 * t] = side(low(a), low(b))
            out[2 * t + 1] = side(high(a), high(b))

    loads[0].wait()
    split(x_ref, x_out)
    loads[1].wait()
    for part in range(2):
        rows = gain_ref[part].astype(f32)
        for i in range(n):
            c = i * HALF
            g_out[i, part : part + 1, :] = side(
                rows[0:1, c : c + HALF], rows[1:2, c : c + HALF]
            )
    pl.semaphore_wait(barrier, n)
    copies = exchange(0, x_out, x_in)
    g_copies = exchange(1, g_out, g_in)
    loads[2].wait()
    split(cot_ref, cot_out)
    cot_copies = exchange(2, cot_out, cot_in)

    loads[3].wait()
    loads[4].wait()
    sub = lax.broadcasted_iota(jnp.int32, (modes, modes), 0)
    lane = lax.broadcasted_iota(jnp.int32, (modes, modes), 1)
    owner_row = jnp.broadcast_to(owner_ref[...], (modes, modes))
    owner_col = jnp.sum(jnp.where(sub == lane, owner_row, 0), axis=1, keepdims=True)
    same = jnp.where((owner_row == owner_col) & (lane < sub), 1, 0)
    slot = owner_col * 2 + jnp.sum(same, axis=1, keepdims=True)
    slot = jnp.broadcast_to(slot, (modes, LANES))
    odd = (lax.broadcasted_iota(jnp.int32, (modes, LANES), 1) >= HALF).astype(jnp.int32)
    masks = [slot == 2 * i + odd for i in range(n)]

    tile = pl.ds(pl.multiple_of((me // 2) * LANES, LANES), LANES)
    parity = lax.rem(me, 2)

    def my_weight(part):
        both = weight_ref[part, :, tile].astype(f32)
        return jnp.where(parity == 1, high(both), low(both))

    w_re, w_im = my_weight(0)[None], my_weight(1)[None]

    def dot(a, b):
        return jnp.dot(a, b, preferred_element_type=f32)

    def apart(values):
        cube = values.reshape(2, modes, modes, HALF)
        return (cube[0], cube[1])

    def joined(re, im):
        rows = modes * modes
        return jnp.concatenate(
            [re.astype(bf16).reshape(rows, HALF), im.astype(bf16).reshape(rows, HALF)], axis=0
        )

    loads[5].wait()
    loads[6].wait()
    for copy in copies:
        copy.wait_recv()
    grid = stack_halves(x_in[...].reshape(n * points, LANES))
    s_re, s_im = apart(dot(table[...], grid))

    for copy in g_copies:
        copy.wait_recv()

    def my_gain(part):
        total = jnp.zeros((modes, LANES), f32)
        for i in range(n):
            row = jnp.broadcast_to(g_in[i, part : part + 1, :], (modes, LANES))
            total = total + jnp.where(masks[i], row, 0.0)
        return (low(total) + high(total))[:, None, :]

    g_re, g_im = my_gain(0), my_gain(1)
    k_re, k_im = complex_product(w_re, w_im, g_re, g_im)

    f_re, f_im = complex_product(s_re, s_im, k_re, k_im)
    field = dot(turned[...], joined(f_re, f_im))
    field = side(field[: n * points], field[n * points :])
    slope = gelu_slope(field)
    for copy in cot_copies:
        copy.wait_recv()
    cot = cot_in[...].reshape(n * points, LANES).astype(f32)
    dfield = stack_halves((cot * slope).astype(bf16))
    d_re, d_im = apart(dot(table[...], dfield))

    h_re = d_re * s_re + d_im * s_im
    h_im = d_im * s_re - d_re * s_im
    wg_re = jnp.sum(h_re * g_re + h_im * g_im, axis=0)
    wg_im = jnp.sum(h_im * g_re - h_re * g_im, axis=0)
    gg_re = jnp.sum(h_re * w_re + h_im * w_im, axis=1)
    gg_im = jnp.sum(h_im * w_re - h_re * w_im, axis=1)
    part_out[0] = side(wg_re, wg_im)
    part_out[1] = side(gg_re, gg_im)
    swap = pltpu.make_async_remote_copy(
        src_ref=part_out,
        dst_ref=part_in,
        send_sem=pair_sem.at[0],
        recv_sem=pair_sem.at[1],
        device_id={"dp": 1 - dp},
        device_id_type=pl.DeviceIdType.MESH,
    )
    swap.start()

    e_re = d_re * k_re + d_im * k_im
    e_im = d_im * k_re - d_re * k_im
    dgrid = dot(turned[...], joined(e_re, e_im))
    dgrid = side(dgrid[: n * points], dgrid[n * points :])
    y_out[...] = (cot + dgrid).astype(bf16).reshape(n, points, LANES)
    y_copies = exchange(3, y_out, y_in)

    swap.wait_recv()
    both_w = (part_out[0] + part_in[0]).astype(bf16)
    both_g = part_out[1] + part_in[1]
    w_out[...] = both_w
    w_copies = []
    for i in order:
        w_copies.append(
            pltpu.make_async_remote_copy(
                src_ref=w_out,
                dst_ref=w_in.at[me],
                send_sem=send_sem.at[4, i],
                recv_sem=recv_sem.at[4, i],
                device_id={"space": peers[i]},
                device_id_type=pl.DeviceIdType.MESH,
            )
        )
    for copy in w_copies:
        copy.start()
    w_in[me] = both_w
    twice = [side(low(both_g), low(both_g)), side(high(both_g), high(both_g))]
    for i in range(n):
        for part in range(2):
            q_out[i, part : part + 1, :] = jnp.sum(
                jnp.where(masks[i], twice[part], 0.0), axis=0, keepdims=True
            )
    q_copies = exchange(5, q_out, q_in)

    for group in (y_copies, w_copies, q_copies):
        for copy in group:
            copy.wait_recv()
    swap.wait_send()
    for group in (copies, g_copies, cot_copies, y_copies, w_copies, q_copies):
        for copy in group:
            copy.wait_send()


def place_kernel(
    n, y_in, w_in, q_in, out_hbm, wgrad_hbm, ggrad_hbm, out_ref, wgrad_ref, ggrad_ref, sem
):
    for t in range(n // 2):
        columns = slice(t * LANES, (t + 1) * LANES)
        a, b = y_in[2 * t], y_in[2 * t + 1]
        out_ref[0, :, columns] = side(low(a), low(b))
        out_ref[1, :, columns] = side(high(a), high(b))
    stores = [pltpu.make_async_copy(out_ref, out_hbm, sem.at[0])]
    stores[0].start()
    for t in range(n // 2):
        columns = slice(t * LANES, (t + 1) * LANES)
        a, b = w_in[2 * t], w_in[2 * t + 1]
        wgrad_ref[0, :, columns] = side(low(a), low(b))
        wgrad_ref[1, :, columns] = side(high(a), high(b))
        a, b = q_in[2 * t], q_in[2 * t + 1]
        first, second = side(low(a), low(b)), side(high(a), high(b))
        for part in range(2):
            ggrad_ref[part, 0:1, columns] = first[part : part + 1]
            ggrad_ref[part, 1:2, columns] = second[part : part + 1]
    stores.append(pltpu.make_async_copy(wgrad_ref, wgrad_hbm, sem.at[1]))
    stores.append(pltpu.make_async_copy(ggrad_ref, ggrad_hbm, sem.at[2]))
    for store in stores[1:]:
        store.start()
    for store in stores:
        store.wait()


def channel_body(n, samples, cotangent, wave_owner, filter_weight, zonal_gain):
    lat_dev, points, channels = samples.shape[1:]
    modes = wave_owner.shape[0]
    table, turned = host_tables(lat_dev * n, points, modes)
    bf16, f32 = jnp.bfloat16, jnp.float32
    vmem = pl.BlockSpec(memory_space=pltpu.VMEM)
    hbm = pl.BlockSpec(memory_space=pltpu.HBM)
    block = pltpu.VMEM((n, points, LANES), bf16)
    small = pltpu.VMEM((n, 2, LANES), f32)
    pair = pltpu.VMEM((2, modes, LANES), f32)
    operands = (
        samples[0],
        cotangent[0],
        wave_owner[None],
        filter_weight,
        zonal_gain,
        jnp.asarray(table),
        jnp.asarray(turned),
    )
    operands = [pltpu.with_memory_space_constraint(x, pltpu.HBM) for x in operands]
    received = pl.pallas_call(
        functools.partial(whole_kernel, n),
        out_shape=(
            pltpu.VMEM((n, points, LANES), bf16),
            pltpu.VMEM((n, modes, LANES), bf16),
            pltpu.VMEM((n, 2, LANES), f32),
        ),
        in_specs=[hbm] * len(operands),
        out_specs=(vmem, vmem, vmem),
        scratch_shapes=[pltpu.VMEM(x.shape, x.dtype) for x in operands]
        + [
            block,
            block,
            block,
            block,
            small,
            small,
            block,
            pair,
            pair,
            pltpu.VMEM((modes, LANES), bf16),
            small,
            pltpu.SemaphoreType.DMA((6, n)),
            pltpu.SemaphoreType.DMA((6, n)),
            pltpu.SemaphoreType.DMA((2,)),
            pltpu.SemaphoreType.DMA((len(operands),)),
        ],
        compiler_params=pltpu.CompilerParams(
            collective_id=0, has_side_effects=True, vmem_limit_bytes=24 * 1024 * 1024
        ),
    )(*operands)
    received = [pltpu.with_memory_space_constraint(x, pltpu.VMEM) for x in received]
    results = (
        jax.ShapeDtypeStruct((lat_dev, points, channels), bf16),
        jax.ShapeDtypeStruct((2, modes, channels), bf16),
        jax.ShapeDtypeStruct((2, zonal_gain.shape[1], channels), f32),
    )
    out, wgrad, ggrad = pl.pallas_call(
        functools.partial(place_kernel, n),
        out_shape=results,
        in_specs=[vmem] * 3,
        out_specs=(hbm, hbm, hbm),
        scratch_shapes=[pltpu.VMEM(x.shape, x.dtype) for x in results]
        + [pltpu.SemaphoreType.DMA((3,))],
        compiler_params=pltpu.CompilerParams(vmem_limit_bytes=8 * 1024 * 1024),
    )(*received)
    return (out[None], wgrad, ggrad)


def body(samples, cotangent, wave_owner, filter_weight, zonal_gain):
    devices = lax.axis_size("space")
    lat_dev, points, channels = samples.shape[1:]
    modes = wave_owner.shape[0]
    fits = (
        lax.axis_size("dp") == 2
        and samples.shape[0] == 1
        and lat_dev == 2
        and zonal_gain.shape[1] == 2
        and channels == devices * HALF
        and devices & (devices - 1) == 0
        and modes % 16 == 0
        and points % 16 == 0
        and modes * modes * devices * points * 16 <= 8 * 1024 * 1024
    )
    if fits:
        return channel_body(devices, samples, cotangent, wave_owner, filter_weight, zonal_gain)
    return general_body(samples, cotangent, wave_owner, filter_weight, zonal_gain)


def solution(mesh):
    in_specs = (
        P(("groups", "dp"), "space", None, None),
        P(("groups", "dp"), "space", None, None),
        P(),
        P(),
        P(None, "space", None),
    )
    out_specs = (
        P(("groups", "dp"), "space", None, None),
        P("groups", None, None),
        P("groups", "space", None),
    )
    return jax.shard_map(body, mesh=mesh, in_specs=in_specs, out_specs=out_specs, check_vma=False)
```

```python
import functools
import math

import jax
import jax.numpy as jnp
import numpy as np
from jax import lax
from jax.experimental import pallas as pl
from jax.experimental.pallas import tpu as pltpu
from jax.sharding import PartitionSpec as P

LANES = 128
HALF = LANES // 2


def slot_tables(wave_owner, per_device, devices):
    is_owner = (wave_owner[:, None] == jnp.arange(devices, dtype=jnp.int32)[None, :]).astype(
        jnp.int32
    )
    owner_rank = jnp.sum((jnp.cumsum(is_owner, axis=0) - 1) * is_owner, axis=1)
    slot_of = wave_owner * per_device + owner_rank
    total_modes = wave_owner.shape[0]
    positions = jnp.arange(total_modes, dtype=jnp.int32)
    matches = (slot_of[None, :] == positions[:, None]).astype(jnp.int32)
    order_of = jnp.sum(matches * positions[None, :], axis=1)
    return (slot_of, order_of)


def fourier_table(wavenums, points):
    longitude = jnp.arange(points, dtype=jnp.int32)
    phase_idx = longitude[:, None] * wavenums[None, :] % points
    angles = phase_idx.astype(jnp.float32) * (2.0 * math.pi / points)
    norm_scale = math.sqrt(2.0 / points)
    return (jnp.stack([jnp.cos(angles), -jnp.sin(angles)], axis=2) * norm_scale).astype(
        jnp.bfloat16
    )


def legendre_table(orders, lat_count, degrees):
    colatitude = (jnp.arange(lat_count, dtype=jnp.float32) + 0.5) * (math.pi / lat_count)
    cosine = jnp.cos(colatitude)
    sine_val = jnp.sin(colatitude)
    log_start = 0.5 * jnp.log((2.0 * orders + 1.0) / (4.0 * math.pi)) + 0.5 * (
        lax.lgamma(2.0 * orders + 1.0) - 2.0 * lax.lgamma(orders + 1.0) - orders * math.log(4.0)
    )
    start_val = jnp.exp(log_start[:, None] + orders[:, None] * jnp.log(sine_val)[None, :])
    quad_weight = math.pi * jnp.sqrt(2.0 * sine_val / lat_count)
    order_col = orders[:, None]

    def advance(carried, degree):
        prev_one, before = carried
        level = degree.astype(jnp.float32)
        is_live = level > order_col
        beyond = level > order_col + 1.0
        lead_coef = jnp.where(
            is_live,
            jnp.sqrt(
                jnp.maximum(4.0 * level * level - 1.0, 0.0)
                / jnp.where(is_live, level * level - order_col * order_col, 1.0)
            ),
            0.0,
        )
        back_num = jnp.maximum((level - 1.0) * (level - 1.0) - order_col * order_col, 0.0)
        back_coef = jnp.where(
            beyond,
            jnp.sqrt(back_num / jnp.where(beyond, 4.0 * (level - 1.0) * (level - 1.0) - 1.0, 1.0)),
            0.0,
        )
        newest = lead_coef * (cosine[None, :] * prev_one - back_coef * before) + jnp.where(
            level == order_col, start_val, 0.0
        )
        return ((newest, prev_one), newest)

    zeros_init = jnp.zeros((orders.shape[0], lat_count), jnp.float32)
    stacked = lax.scan(
        advance, (zeros_init, zeros_init), jnp.arange(degrees, dtype=jnp.int32), unroll=16
    )[1]
    return jnp.transpose(stacked, (1, 0, 2)) * quad_weight[None, None, :]


def gelu_slope(values):
    return (
        0.5 * (1.0 + lax.erf(values * 0.7071067811865476))
        + values * jnp.exp(-0.5 * values * values) * 0.3989422804014327
    )


def complex_product(left_re, left_im, right_re, right_im):
    return (left_re * right_re - left_im * right_im, left_re * right_im + left_im * right_re)


def analysis(legendre, columns):
    return jnp.einsum("ilj,ijrc->ilrc", legendre, columns, preferred_element_type=jnp.float32)


def synthesis(legendre, spectra):
    return jnp.einsum("ilj,ilrc->ijrc", legendre, spectra, preferred_element_type=jnp.float32)


def general_body(samples, cotangent, wave_owner, filter_weight, zonal_gain):
    devices = lax.axis_size("space")
    own_index = lax.axis_index("space")
    per_device = zonal_gain.shape[1]
    total_modes = wave_owner.shape[0]
    points = samples.shape[2]
    slot_of, order_of = slot_tables(wave_owner, per_device, devices)
    mine = lax.dynamic_slice_in_dim(order_of, own_index * per_device, per_device)
    table = fourier_table(order_of, points)
    legendre = legendre_table(mine.astype(jnp.float32), total_modes, total_modes).astype(
        jnp.bfloat16
    )
    grid = samples[0]
    cot_grid = cotangent[0]
    weight_re = filter_weight[0].astype(jnp.float32)[None]
    weight_im = filter_weight[1].astype(jnp.float32)[None]
    gain_re = zonal_gain[0].astype(jnp.float32)[:, None, :]
    gain_im = zonal_gain[1].astype(jnp.float32)[:, None, :]
    kern_re, kern_im = complex_product(weight_re, weight_im, gain_re, gain_im)
    fourier = jnp.einsum("jkc,ksr->sjrc", grid, table, preferred_element_type=jnp.float32).astype(
        jnp.bfloat16
    )
    owned = lax.all_to_all(fourier, "space", split_axis=0, concat_axis=1, tiled=True)
    spectral = analysis(legendre, owned)
    spec_re = spectral[:, :, 0]
    spec_im = spectral[:, :, 1]
    filt_re, filt_im = complex_product(spec_re, spec_im, kern_re, kern_im)
    filtered = jnp.stack([filt_re, filt_im], axis=2).astype(jnp.bfloat16)
    zonal = synthesis(legendre, filtered).astype(jnp.bfloat16)
    banded = lax.all_to_all(zonal, "space", split_axis=1, concat_axis=0, tiled=True)
    field = jnp.einsum("sjrc,ksr->jkc", banded, table, preferred_element_type=jnp.float32)
    dfield = (cot_grid.astype(jnp.float32) * gelu_slope(field)).astype(jnp.bfloat16)
    dzonal = jnp.einsum("jkc,ksr->sjrc", dfield, table, preferred_element_type=jnp.float32).astype(
        jnp.bfloat16
    )
    grad_owned = lax.all_to_all(dzonal, "space", split_axis=0, concat_axis=1, tiled=True)
    dfiltered = analysis(legendre, grad_owned)
    grad_re = dfiltered[:, :, 0]
    grad_im = dfiltered[:, :, 1]
    prod_re, prod_im = complex_product(spec_re, spec_im, gain_re, gain_im)
    weight_part = jnp.stack(
        [
            jnp.sum(grad_re * prod_re + grad_im * prod_im, axis=0),
            jnp.sum(grad_im * prod_re - grad_re * prod_im, axis=0),
        ]
    )
    other_re, other_im = complex_product(spec_re, spec_im, weight_re, weight_im)
    gain_part = jnp.stack(
        [
            jnp.sum(grad_re * other_re + grad_im * other_im, axis=1),
            jnp.sum(grad_im * other_re - grad_re * other_im, axis=1),
        ]
    )
    dspec = jnp.stack(
        [grad_re * kern_re + grad_im * kern_im, grad_im * kern_re - grad_re * kern_im], axis=2
    ).astype(jnp.bfloat16)
    dfourier = synthesis(legendre, dspec).astype(jnp.bfloat16)
    grad_banded = lax.all_to_all(dfourier, "space", split_axis=1, concat_axis=0, tiled=True)
    sample_grad = (
        cot_grid.astype(jnp.float32)
        + jnp.einsum("sjrc,ksr->jkc", grad_banded, table, preferred_element_type=jnp.float32)
    ).astype(jnp.bfloat16)
    weight_grad = lax.psum(weight_part, ("dp", "space")).astype(jnp.bfloat16)
    gain_grad = lax.psum(gain_part, "dp")
    return (sample_grad[None], weight_grad, gain_grad)


def host_tables(lats, points, modes):
    m = np.arange(modes, dtype=np.float64)
    angles = (np.arange(points)[:, None] * np.arange(modes)[None, :] % points) * (
        2.0 * math.pi / points
    )
    fourier = np.stack([np.cos(angles), -np.sin(angles)]) * math.sqrt(2.0 / points)
    fourier = fourier.astype(np.float32).astype(jnp.bfloat16).astype(np.float64)
    colat = (np.arange(lats) + 0.5) * (math.pi / lats)
    cosine, sine = np.cos(colat), np.sin(colat)
    log_start = np.array(
        [
            0.5 * math.log((2 * o + 1) / (4 * math.pi))
            + 0.5 * (math.lgamma(2 * o + 1) - 2 * math.lgamma(o + 1) - o * math.log(4.0))
            for o in range(modes)
        ]
    )
    pbar = np.zeros((modes, modes, lats))
    for o in range(modes):
        pbar[o, o] = np.exp(log_start[o] + m[o] * np.log(sine))
        for l in range(o + 1, modes):
            lead = math.sqrt((4 * l * l - 1) / (l * l - o * o))
            pbar[o, l] = lead * cosine * pbar[o, l - 1]
            if l > o + 1:
                back = math.sqrt(((l - 1) ** 2 - o * o) / (4 * (l - 1) ** 2 - 1))
                pbar[o, l] -= lead * back * pbar[o, l - 2]
    legendre = pbar * (math.pi * np.sqrt(2.0 * sine / lats))[None, None, :]
    legendre = legendre.astype(np.float32).astype(jnp.bfloat16).astype(np.float64)
    table = np.einsum("mlj,rkm->rmljk", legendre, fourier)
    table = table.reshape(2, modes, modes, lats // 2, 2, points).transpose(0, 1, 2, 4, 3, 5)
    table = table.reshape(2 * modes * modes, lats * points).astype(np.float32)
    return (table.astype(jnp.bfloat16), np.ascontiguousarray(table.T).astype(jnp.bfloat16))


def low(values):
    return values[:, :HALF]


def high(values):
    return values[:, HALF:]


def side(left, right):
    return jnp.concatenate([left, right], axis=1)


def stack_halves(values):
    return jnp.concatenate([low(values), high(values)], axis=0)


def whole_kernel(
    n,
    x_hbm,
    cot_hbm,
    owner_hbm,
    weight_hbm,
    gain_hbm,
    table_hbm,
    turned_hbm,
    y_in,
    w_in,
    q_in,
    x_ref,
    cot_ref,
    owner_ref,
    weight_ref,
    gain_ref,
    table,
    turned,
    x_out,
    x_in,
    cot_out,
    cot_in,
    y_out,
    part_out,
    part_in,
    w_out,
    q_out,
    send_sem,
    recv_sem,
    pair_sem,
    load_sem,
):
    f32, bf16 = jnp.float32, jnp.bfloat16
    me = lax.axis_index("space")
    dp = lax.axis_index("dp")
    points = x_ref.shape[1]
    modes = weight_ref.shape[1]
    peers = [me ^ i for i in range(n)]
    order = list(range(n - 1, 0, -1))

    barrier = pltpu.get_barrier_semaphore()
    for i in order:
        pl.semaphore_signal(
            barrier, inc=1, device_id={"space": peers[i]}, device_id_type=pl.DeviceIdType.MESH
        )
    pl.semaphore_signal(
        barrier, inc=1, device_id={"dp": 1 - dp}, device_id_type=pl.DeviceIdType.MESH
    )
    loads = [
        pltpu.make_async_copy(source, target, load_sem.at[i])
        for i, (source, target) in enumerate(
            [
                (x_hbm, x_ref),
                (gain_hbm, gain_ref),
                (cot_hbm, cot_ref),
                (owner_hbm, owner_ref),
                (weight_hbm, weight_ref),
                (table_hbm, table),
                (turned_hbm, turned),
            ]
        )
    ]
    for load in loads:
        load.start()
    def exchange(kind, source, target):
        copies = []
        for i in order:
            copies.append(
                pltpu.make_async_remote_copy(
                    src_ref=source.at[peers[i]],
                    dst_ref=target.at[me],
                    send_sem=send_sem.at[kind, i],
                    recv_sem=recv_sem.at[kind, i],
                    device_id={"space": peers[i]},
                    device_id_type=pl.DeviceIdType.MESH,
                )
            )
        for copy in copies:
            copy.start()
        target[me] = source[me]
        return copies

    def split(ref, out):
        first, second = ref[0], ref[1]
        for t in range(n // 2):
            a = first[:, t * LANES : (t + 1) * LANES]
            b = second[:, t * LANES : (t + 1) * LANES]
            out[2 * t, 0:points] = side(low(a), low(b))
            out[2 * t + 1, 0:points] = side(high(a), high(b))

    loads[0].wait()
    split(x_ref, x_out)
    loads[1].wait()
    rows = [gain_ref[part].astype(f32) for part in range(2)]
    for i in range(n):
        c = slice(i * HALF, (i + 1) * HALF)
        x_out[i, points : points + 16, :] = jnp.concatenate(
            [side(row[0:1, c], row[1:2, c]) for row in rows] + [jnp.zeros((14, LANES), f32)],
            axis=0,
        ).astype(bf16)
    pl.semaphore_wait(barrier, n)
    copies = exchange(0, x_out, x_in)
    loads[2].wait()
    split(cot_ref, cot_out)
    cot_copies = exchange(1, cot_out, cot_in)

    loads[3].wait()
    loads[4].wait()
    sub = lax.broadcasted_iota(jnp.int32, (modes, modes), 0)
    lane = lax.broadcasted_iota(jnp.int32, (modes, modes), 1)
    owner_row = jnp.broadcast_to(owner_ref[...], (modes, modes))
    owner_col = jnp.sum(jnp.where(sub == lane, owner_row, 0), axis=1, keepdims=True)
    same = jnp.where((owner_row == owner_col) & (lane < sub), 1, 0)
    slot = owner_col * 2 + jnp.sum(same, axis=1, keepdims=True)
    slot = jnp.broadcast_to(slot, (modes, LANES))
    odd = (lax.broadcasted_iota(jnp.int32, (modes, LANES), 1) >= HALF).astype(jnp.int32)
    masks = [slot == 2 * i + odd for i in range(n)]

    tile = pl.ds(pl.multiple_of((me // 2) * LANES, LANES), LANES)
    parity = lax.rem(me, 2)

    def my_weight(part):
        both = weight_ref[part, :, tile].astype(f32)
        return jnp.where(parity == 1, high(both), low(both))

    w_re, w_im = my_weight(0)[None], my_weight(1)[None]

    def dot(a, b):
        return jnp.dot(a, b, preferred_element_type=f32)

    def apart(values):
        cube = values.reshape(2, modes, modes, HALF)
        return (cube[0], cube[1])

    def joined(re, im):
        rows = modes * modes
        return jnp.concatenate(
            [re.astype(bf16).reshape(rows, HALF), im.astype(bf16).reshape(rows, HALF)], axis=0
        )

    loads[5].wait()
    loads[6].wait()
    for copy in copies:
        copy.wait_recv()
    grid = stack_halves(x_in[:, 0:points].reshape(n * points, LANES))
    s_re, s_im = apart(dot(table[...], grid))

    gain_rows = [x_in[i, points : points + 16].astype(f32) for i in range(n)]

    def my_gain(part):
        total = jnp.zeros((modes, LANES), f32)
        for i in range(n):
            row = jnp.broadcast_to(gain_rows[i][part : part + 1], (modes, LANES))
            total = total + jnp.where(masks[i], row, 0.0)
        return (low(total) + high(total))[:, None, :]

    g_re, g_im = my_gain(0), my_gain(1)
    k_re, k_im = complex_product(w_re, w_im, g_re, g_im)

    f_re, f_im = complex_product(s_re, s_im, k_re, k_im)
    field = dot(turned[...], joined(f_re, f_im))
    field = side(field[: n * points], field[n * points :])
    slope = gelu_slope(field)
    for copy in cot_copies:
        copy.wait_recv()
    cot = cot_in[...].reshape(n * points, LANES).astype(f32)
    dfield = stack_halves((cot * slope).astype(bf16))
    d_re, d_im = apart(dot(table[...], dfield))

    h_re = d_re * s_re + d_im * s_im
    h_im = d_im * s_re - d_re * s_im
    wg_re = jnp.sum(h_re * g_re + h_im * g_im, axis=0)
    wg_im = jnp.sum(h_im * g_re - h_re * g_im, axis=0)
    part_out[0] = side(wg_re, wg_im)

    def swap(i):
        return pltpu.make_async_remote_copy(
            src_ref=part_out.at[i],
            dst_ref=part_in.at[i],
            send_sem=pair_sem.at[0, i],
            recv_sem=pair_sem.at[1, i],
            device_id={"dp": 1 - dp},
            device_id_type=pl.DeviceIdType.MESH,
        )

    swaps = [swap(0), swap(1)]
    swaps[0].start()
    gg_re = jnp.sum(h_re * w_re + h_im * w_im, axis=1)
    gg_im = jnp.sum(h_im * w_re - h_re * w_im, axis=1)
    twice = [side(gg_re, gg_re), side(gg_im, gg_im)]
    part_out[1] = jnp.concatenate(
        [
            jnp.sum(jnp.where(masks[i], twice[part], 0.0), axis=0, keepdims=True)
            for i in range(n)
            for part in range(2)
        ],
        axis=0,
    )
    swaps[1].start()

    e_re = d_re * k_re + d_im * k_im
    e_im = d_im * k_re - d_re * k_im
    dgrid = dot(turned[...], joined(e_re, e_im))
    dgrid = side(dgrid[: n * points], dgrid[n * points :])
    y_out[...] = (cot + dgrid).astype(bf16).reshape(n, points, LANES)
    y_copies = exchange(2, y_out, y_in)

    swaps[0].wait_recv()
    both_w = (part_out[0] + part_in[0]).astype(bf16)
    w_out[...] = both_w
    w_copies = []
    for i in order:
        w_copies.append(
            pltpu.make_async_remote_copy(
                src_ref=w_out,
                dst_ref=w_in.at[me],
                send_sem=send_sem.at[3, i],
                recv_sem=recv_sem.at[3, i],
                device_id={"space": peers[i]},
                device_id_type=pl.DeviceIdType.MESH,
            )
        )
    for copy in w_copies:
        copy.start()
    w_in[me] = both_w
    swaps[1].wait_recv()
    q_out[...] = (part_out[1] + part_in[1]).reshape(n, 2, LANES)
    q_copies = exchange(4, q_out, q_in)

    for group in (y_copies, w_copies, q_copies):
        for copy in group:
            copy.wait_recv()
    for swapped in swaps:
        swapped.wait_send()
    for group in (copies, cot_copies, y_copies, w_copies, q_copies):
        for copy in group:
            copy.wait_send()


def place_kernel(
    n, y_in, w_in, q_in, out_hbm, wgrad_hbm, ggrad_hbm, out_ref, wgrad_ref, ggrad_ref, sem
):
    for t in range(n // 2):
        columns = slice(t * LANES, (t + 1) * LANES)
        a, b = y_in[2 * t], y_in[2 * t + 1]
        out_ref[0, :, columns] = side(low(a), low(b))
        out_ref[1, :, columns] = side(high(a), high(b))
    stores = [pltpu.make_async_copy(out_ref, out_hbm, sem.at[0])]
    stores[0].start()
    for t in range(n // 2):
        columns = slice(t * LANES, (t + 1) * LANES)
        a, b = w_in[2 * t], w_in[2 * t + 1]
        wgrad_ref[0, :, columns] = side(low(a), low(b))
        wgrad_ref[1, :, columns] = side(high(a), high(b))
        a, b = q_in[2 * t], q_in[2 * t + 1]
        first, second = side(low(a), low(b)), side(high(a), high(b))
        for part in range(2):
            ggrad_ref[part, 0:1, columns] = first[part : part + 1]
            ggrad_ref[part, 1:2, columns] = second[part : part + 1]
    stores.append(pltpu.make_async_copy(wgrad_ref, wgrad_hbm, sem.at[1]))
    stores.append(pltpu.make_async_copy(ggrad_ref, ggrad_hbm, sem.at[2]))
    for store in stores[1:]:
        store.start()
    for store in stores:
        store.wait()


def channel_body(n, samples, cotangent, wave_owner, filter_weight, zonal_gain):
    lat_dev, points, channels = samples.shape[1:]
    modes = wave_owner.shape[0]
    table, turned = host_tables(lat_dev * n, points, modes)
    bf16, f32 = jnp.bfloat16, jnp.float32
    vmem = pl.BlockSpec(memory_space=pltpu.VMEM)
    hbm = pl.BlockSpec(memory_space=pltpu.HBM)
    block = pltpu.VMEM((n, points, LANES), bf16)
    tall = pltpu.VMEM((n, points + 16, LANES), bf16)
    small = pltpu.VMEM((n, 2, LANES), f32)
    pair = pltpu.VMEM((2, modes, LANES), f32)
    operands = (
        samples[0],
        cotangent[0],
        wave_owner[None],
        filter_weight,
        zonal_gain,
        jnp.asarray(table),
        jnp.asarray(turned),
    )
    operands = [pltpu.with_memory_space_constraint(x, pltpu.HBM) for x in operands]
    received = pl.pallas_call(
        functools.partial(whole_kernel, n),
        out_shape=(
            pltpu.VMEM((n, points, LANES), bf16),
            pltpu.VMEM((n, modes, LANES), bf16),
            pltpu.VMEM((n, 2, LANES), f32),
        ),
        in_specs=[hbm] * len(operands),
        out_specs=(vmem, vmem, vmem),
        scratch_shapes=[pltpu.VMEM(x.shape, x.dtype) for x in operands]
        + [
            tall,
            tall,
            block,
            block,
            block,
            pair,
            pair,
            pltpu.VMEM((modes, LANES), bf16),
            small,
            pltpu.SemaphoreType.DMA((5, n)),
            pltpu.SemaphoreType.DMA((5, n)),
            pltpu.SemaphoreType.DMA((2, 2)),
            pltpu.SemaphoreType.DMA((len(operands),)),
        ],
        compiler_params=pltpu.CompilerParams(
            collective_id=0, has_side_effects=True, vmem_limit_bytes=24 * 1024 * 1024
        ),
    )(*operands)
    received = [pltpu.with_memory_space_constraint(x, pltpu.VMEM) for x in received]
    results = (
        jax.ShapeDtypeStruct((lat_dev, points, channels), bf16),
        jax.ShapeDtypeStruct((2, modes, channels), bf16),
        jax.ShapeDtypeStruct((2, zonal_gain.shape[1], channels), f32),
    )
    out, wgrad, ggrad = pl.pallas_call(
        functools.partial(place_kernel, n),
        out_shape=results,
        in_specs=[vmem] * 3,
        out_specs=(hbm, hbm, hbm),
        scratch_shapes=[pltpu.VMEM(x.shape, x.dtype) for x in results]
        + [pltpu.SemaphoreType.DMA((3,))],
        compiler_params=pltpu.CompilerParams(vmem_limit_bytes=8 * 1024 * 1024),
    )(*received)
    return (out[None], wgrad, ggrad)


def body(samples, cotangent, wave_owner, filter_weight, zonal_gain):
    devices = lax.axis_size("space")
    lat_dev, points, channels = samples.shape[1:]
    modes = wave_owner.shape[0]
    fits = (
        lax.axis_size("dp") == 2
        and samples.shape[0] == 1
        and lat_dev == 2
        and zonal_gain.shape[1] == 2
        and channels == devices * HALF
        and devices & (devices - 1) == 0
        and modes % 16 == 0
        and points % 16 == 0
        and modes * modes * devices * points * 16 <= 8 * 1024 * 1024
    )
    if fits:
        return channel_body(devices, samples, cotangent, wave_owner, filter_weight, zonal_gain)
    return general_body(samples, cotangent, wave_owner, filter_weight, zonal_gain)


def solution(mesh):
    in_specs = (
        P(("groups", "dp"), "space", None, None),
        P(("groups", "dp"), "space", None, None),
        P(),
        P(),
        P(None, "space", None),
    )
    out_specs = (
        P(("groups", "dp"), "space", None, None),
        P("groups", None, None),
        P("groups", "space", None),
    )
    return jax.shard_map(body, mesh=mesh, in_specs=in_specs, out_specs=out_specs, check_vma=False)
```
